32 devices in a mesh: ctx: 8 (over z, y), seq: 2 (over x), wsh: 2 (over core).
Axes of the slice: x: 2, y: 2, z: 4, core: 2. Of those that a mesh axis runs over, the one named last changes fastest.
Arguments:
- tokens: bfloat16 [4, 1024, 1024], P(('seq', 'wsh'), 'ctx'), may hold values from -6 to 6
- positions: int32 [4, 1024], P(('seq', 'wsh'), 'ctx'), may hold values from 0 to 895, as said below
- w_qkv: bfloat16 [1024, 3072], P(('seq', 'wsh')), may hold values from -0.1875 to 0.1875
- w_out: bfloat16 [1024, 1024], P(('seq', 'wsh')), may hold values from -3.5 to 3.5
- w_in: bfloat16 [1024, 5248], P(('seq', 'wsh')), may hold values from -0.1875 to 0.1875
- w_down: bfloat16 [2624, 1024], P(('seq', 'wsh')), may hold values from -0.125 to 0.125
- gain_attn: bfloat16 [1024], P(('seq', 'wsh')), may hold values from 0.099609375 to 1.8984375
- gain_mlp: bfloat16 [1024], P(('seq', 'wsh')), may hold values from 0.099609375 to 1.8984375
- cotangent: bfloat16 [4, 1024, 1024], P(('seq', 'wsh'), 'ctx'), may hold values from -6 to 6
Outputs:
- output: bfloat16 [4, 1024, 1024], P(('seq', 'wsh'), 'ctx')
- grad_tokens: bfloat16 [4, 1024, 1024], P(('seq', 'wsh'), 'ctx')
- grad_w_qkv: float32 [1024, 3072], P(('seq', 'wsh'))
- grad_w_out: float32 [1024, 1024], P(('seq', 'wsh'))
- grad_w_in: float32 [1024, 5248], P(('seq', 'wsh'))
- down_weight_gradient: float32 [2624, 1024], P(('seq', 'wsh'))
- grad_gain_attn: float32 [1024], P(('seq', 'wsh'))
- grad_gain_mlp: float32 [1024], P(('seq', 'wsh'))
The draws below stay inside these ranges and needn't reach their ends.
Inputs may be any that keep to these rules, and one draw needn't show every extreme that they name: Each sequence is a run of packed documents: positions count 0, 1, 2 and so on from the first token of each document. Every sequence holds one document of exactly 1024 - 128 tokens, which begins after the sequence's first token and within its first 128 tokens; the tokens before and after it form one or more shorter documents.
All inputs are finite; a program needn't handle non-finite values.
Results may differ from the reference program's by a relative error of at most 0.02.
Values may be sent and summed in bfloat16 or wider, within the bound.
A program may use at most 192 MiB of HBM per device.

```python
import math
import jax
import jax.numpy as jnp
from jax import lax

D = 1024
HEADS = 16
HEAD = 64
FF = 2624
TOK_SEQ = 128
LENGTH = 1024
SEQS = 4


def draw_positions(key, part):
    key = jax.random.fold_in(key, 11)
    first_key, second_key = jax.random.split(key)
    index_row = jnp.arange(LENGTH, dtype=jnp.int32)[None, :]
    long_start = jax.random.randint(second_key, (SEQS, 1), 1, TOK_SEQ).astype(jnp.int32)
    long_end = long_start + (LENGTH - TOK_SEQ)
    inside = (index_row >= long_start) & (index_row < long_end)
    starts_at = jax.random.randint(first_key, (SEQS, LENGTH), 0, 8) == 0
    starts_at = starts_at & jnp.logical_not(inside) | (index_row == 0) | (index_row == long_start) | (index_row == long_end)
    marked = jnp.where(starts_at, index_row, 0).astype(jnp.int32)
    doc_start = lax.cummax(marked, axis=1)
    return (index_row - doc_start).astype(jnp.int32)


def steps_of(own_key, dims, cuts, smallest, largest):
    factor_of = 1.0
    for axis_at, parts in cuts:
        draws = jax.random.uniform(jax.random.fold_in(jax.random.fold_in(own_key, 6), axis_at), (parts,), jnp.float32, smallest / len(cuts), largest / len(cuts))
        factor_of = factor_of * jnp.repeat(jnp.exp(draws), dims[axis_at] // parts).reshape((-1,) + (1,) * (len(dims) - 1 - axis_at))
    return factor_of


def normal_values(rng, dims, width, bound, cuts=(), kind=jnp.bfloat16):
    entries = jax.random.normal(rng, dims, jnp.float32) * width
    if len(cuts) > 0:
        entries = steps_of(rng, dims, cuts, -0.22, 0.18) * entries
    return jnp.clip(entries, min=-bound, max=bound).astype(kind)


def setup_inputs(seed: int = 0) -> dict:
    streams_of = jax.random.split(jax.random.key(seed), 10)
    tokens = normal_values(streams_of[0], (SEQS, LENGTH, D), 1.0, 6.0, ((0, 4), (1, 8)))
    positions = draw_positions(jax.random.fold_in(streams_of[9], 71), 0)
    w_qkv = normal_values(streams_of[2], (D, 3 * D), D ** -0.5, 0.1875, ((0, 4),))
    w_out = normal_values(streams_of[3], (D, D), (max(1, 3 * D // LENGTH)) ** -0.5, 3.5, ((0, 4),))
    w_in = normal_values(streams_of[4], (D, 2 * FF), D ** -0.5, 0.1875, ((0, 4),))
    w_down = normal_values(streams_of[5], (FF, D), FF ** -0.5, 0.125, ((0, 4),))
    gain_attn = jnp.clip(1.0 + 0.18 * jax.random.normal(streams_of[6], (D,), jnp.float32), 0.099609375, 1.8984375).astype(jnp.bfloat16)
    gain_mlp = jnp.clip(1.0 + 0.18 * jax.random.normal(streams_of[7], (D,), jnp.float32), 0.099609375, 1.8984375).astype(jnp.bfloat16)
    cotangent = normal_values(streams_of[8], (SEQS, LENGTH, D), 1.0, 6.0, ((0, 4), (1, 8)))
    return dict(tokens=tokens, positions=positions, w_qkv=w_qkv, w_out=w_out, w_in=w_in, w_down=w_down, gain_attn=gain_attn, gain_mlp=gain_mlp, cotangent=cotangent)


layer_eps = 1e-05
rope_base = 160000.0
far_below = -1e+30

@jax.custom_vjp
def low(v):
    return lax.optimization_barrier(v.astype(jnp.bfloat16)).astype(jnp.float32)

@jax.custom_vjp
def low_back(v):
    return v

def low_keep(v):
    return (low(v), None)

def low_pass(kept, grad):
    return (grad,)

def back_keep(v):
    return (v, None)

def back_low(kept, grad):
    return (low(grad),)
low.defvjp(low_keep, low_pass)
low_back.defvjp(back_keep, back_low)

def normalize(values, gain_vector):
    middle = lax.optimization_barrier(jnp.mean(values, -1, keepdims=True))
    centred = values - middle
    spread = lax.optimization_barrier(jnp.mean(centred * centred, -1, keepdims=True))
    return centred * lax.rsqrt(spread + layer_eps) * gain_vector

def rotary_tables(positions):
    half_size = HEAD // 2
    frequency = jnp.exp(jnp.arange(half_size, dtype=jnp.float32) * (-2.0 * math.log(rope_base) / HEAD))
    angles = positions.astype(jnp.float32)[..., None] * frequency
    cosine = jnp.cos(angles)
    sine_table = jnp.sin(angles)
    return (jnp.concatenate([cosine, cosine], -1)[..., None, :], jnp.concatenate([sine_table, sine_table], -1)[..., None, :])

def rotate(values, cosine, sine_table):
    half_size = values.shape[-1] // 2
    turned = jnp.concatenate([-values[..., half_size:], values[..., :half_size]], -1)
    return values * cosine + turned * sine_table

def geglu(inner_part, gate_part):
    return jax.nn.gelu(inner_part, approximate=False) * gate_part

def attend(queries, key_rows, value_rows, doc_starts):
    block_size = math.gcd(LENGTH, 512)
    scaling = HEAD ** (-0.5)

    def one_sequence(quad):
        seq_queries, seq_keys, seq_values, seq_starts = quad

        def one_block(pair):
            query_block, start_block = pair
            same_doc = (start_block[:, None] == seq_starts[None, :])[:, None, :]
            scores = low_back(jnp.einsum('qhd,khd->qhk', query_block, seq_keys, precision=lax.Precision.HIGHEST) * scaling)
            masked = jnp.where(same_doc, scores, far_below)
            best_score = lax.optimization_barrier(jnp.max(masked, -1, keepdims=True))
            raised = jnp.where(same_doc, jnp.exp(masked - best_score), 0.0)
            weights_low = low(raised / lax.optimization_barrier(jnp.sum(raised, -1, keepdims=True)))
            return jnp.einsum('qhk,khd->qhd', weights_low, seq_values, precision=lax.Precision.HIGHEST)
        blocks = seq_queries.reshape(LENGTH // block_size, block_size, HEADS, HEAD)
        start_blocks = seq_starts.reshape(LENGTH // block_size, block_size)
        return lax.map(jax.checkpoint(one_block), (blocks, start_blocks)).reshape(LENGTH, HEADS, HEAD)
    return lax.map(jax.checkpoint(one_sequence), (queries, key_rows, value_rows, doc_starts))

def forward(input_widened, cosine, sine_table, doc_starts, query_key_value_weight, out_weight_widened, in_weight_widened, down_weight_widened, gain_one, gain_two):
    highest_precision = lax.Precision.HIGHEST
    attention_normed = low(normalize(input_widened, gain_one))
    projected_output = low_back(jnp.einsum('kch,hf->kcf', attention_normed, query_key_value_weight, precision=highest_precision))
    split_shape = input_widened.shape[:2] + (HEADS, HEAD)
    queries = low(rotate(projected_output[..., :D].reshape(split_shape), cosine, sine_table))
    key_rows = low(rotate(projected_output[..., D:2 * D].reshape(split_shape), cosine, sine_table))
    value_rows = low(projected_output[..., 2 * D:].reshape(split_shape))
    attended = attend(queries, key_rows, value_rows, doc_starts).reshape(input_widened.shape)
    attended_reduced = low_back(low(attended))
    mixed_token_rows = input_widened + low_back(jnp.einsum('kch,hf->kcf', attended_reduced, out_weight_widened, precision=highest_precision))
    feedforward_normed = low(normalize(mixed_token_rows, gain_two))
    hidden_state = low_back(jnp.einsum('rnk,kx->rnx', feedforward_normed, in_weight_widened, precision=highest_precision))
    gated_product = low(geglu(hidden_state[..., :FF], hidden_state[..., FF:]))
    return mixed_token_rows + jnp.einsum('ogw,wn->ogn', gated_product, down_weight_widened, precision=highest_precision)

def reference(tokens, positions, w_qkv, w_out, w_in, w_down, gain_attn, gain_mlp, cotangent):
    group_size = math.gcd(SEQS, max(1, 4096 // LENGTH))
    group_count = SEQS // group_size
    weights_f = tuple((w.astype(jnp.float32) for w in (w_qkv, w_out, w_in, w_down, gain_attn, gain_mlp)))

    def one_group(totals, slices):
        group_tokens, group_positions, group_cot = slices
        cosine, sine_table = rotary_tables(group_positions)
        doc_starts = (jnp.arange(LENGTH, dtype=jnp.int32)[None, :] - group_positions).astype(jnp.int32)

        def layer(input_widened, query_key_value_weight, out_weight_widened, in_weight_widened, down_weight_widened, gain_one, gain_two):
            return forward(input_widened, cosine, sine_table, doc_starts, query_key_value_weight, out_weight_widened, in_weight_widened, down_weight_widened, gain_one, gain_two)
        result, pull = jax.vjp(layer, group_tokens.astype(jnp.float32), *weights_f)
        grads = pull(group_cot.astype(jnp.float32))
        totals = tuple((total + grad for total, grad in zip(totals, grads[1:])))
        return (totals, (result.astype(jnp.bfloat16), grads[0].astype(jnp.bfloat16)))
    start_totals = tuple((jnp.zeros_like(w) for w in weights_f))
    shaped = (tokens.reshape(group_count, group_size, LENGTH, D), positions.reshape(group_count, group_size, LENGTH), cotangent.reshape(group_count, group_size, LENGTH, D))
    totals, (results, grad_inputs) = lax.scan(one_group, start_totals, shaped)
    return (results.reshape(SEQS, LENGTH, D), grad_inputs.reshape(SEQS, LENGTH, D), totals[0], totals[1], totals[2], totals[3], totals[4], totals[5])
```

```python
import functools
import math

import jax
import jax.numpy as jnp
from jax import lax
from jax.experimental import pallas as pl
from jax.experimental.pallas import tpu as pltpu
from jax.sharding import PartitionSpec as P

D = 1024
HEADS = 16
HEAD = 64
FF = 2624


layer_eps = 1e-05
rope_base = 160000.0
far_below = -1e30


def from_behind(shard, axis, by):
    size = lax.axis_size(axis)
    return lax.ppermute(shard, axis, [(i, (i + by) % size) for i in range(size)])


def normalize(values, gain_vector):
    middle = jnp.mean(values, -1, keepdims=True)
    centred = values - middle
    spread = jnp.mean(centred * centred, -1, keepdims=True)
    return centred * lax.rsqrt(spread + layer_eps) * gain_vector


def rotary_tables(positions):
    half_size = HEAD // 2
    frequency = jnp.exp(
        jnp.arange(half_size, dtype=jnp.float32) * (-2.0 * math.log(rope_base) / HEAD)
    )
    angles = positions.astype(jnp.float32)[..., None] * frequency
    cosine = jnp.cos(angles)
    sine_table = jnp.sin(angles)
    return (
        jnp.concatenate([cosine, cosine], -1)[..., None, :],
        jnp.concatenate([sine_table, sine_table], -1)[..., None, :],
    )


def rotate(values, cosine, sine_table):
    half_size = values.shape[-1] // 2
    turned = jnp.concatenate([-values[..., half_size:], values[..., :half_size]], -1)
    return values * cosine + turned * sine_table


def rotate_back(grads, cosine, sine_table):
    half_size = grads.shape[-1] // 2
    shifted = grads * sine_table
    return grads * cosine + jnp.concatenate(
        [shifted[..., half_size:], -shifted[..., :half_size]], -1
    )


def geglu(inner_part, gate_part):
    return jax.nn.gelu(inner_part, approximate=False) * gate_part


def same_document(query_starts, key_starts):
    return (query_starts[:, :, None] == key_starts[:, None, :])[:, :, None, :]


def fold_keys(queries, query_starts, scaling, running, piece):
    key_piece, value_piece, start_piece = piece
    seq_count = key_piece.shape[0]
    row_total = key_piece.shape[1]
    block_size = math.gcd(row_total, 512)

    def one_block(block_index, carried):
        best_score, totals, weighted = carried
        key_block = lax.dynamic_slice_in_dim(
            key_piece, block_index * block_size, block_size, 1
        ).reshape(seq_count, block_size, HEADS, HEAD)
        value_block = lax.dynamic_slice_in_dim(
            value_piece, block_index * block_size, block_size, 1
        ).reshape(seq_count, block_size, HEADS, HEAD)
        start_block = lax.dynamic_slice_in_dim(start_piece, block_index * block_size, block_size, 1)
        same_doc = same_document(query_starts, start_block)
        scores = (
            jnp.einsum("sqhd,skhd->sqhk", queries, key_block, preferred_element_type=jnp.float32)
            * scaling
        )
        scores = jnp.where(same_doc, scores, far_below)
        new_best = jnp.maximum(best_score, jnp.max(scores, -1))
        fading = jnp.exp(best_score - new_best)
        raised = jnp.where(same_doc, jnp.exp(scores - new_best[..., None]), 0.0)
        totals = totals * fading + jnp.sum(raised, -1)
        weighted = weighted * fading[..., None] + jnp.einsum(
            "sqhk,skhd->sqhd",
            raised.astype(jnp.bfloat16),
            value_block,
            preferred_element_type=jnp.float32,
        )
        return (new_best, totals, weighted)

    return lax.fori_loop(0, row_total // block_size, one_block, running)


def block_grads(
    queries,
    query_starts,
    key_block,
    value_block,
    key_starts,
    grad_split,
    log_total,
    row_dot,
    scaling,
):
    same_doc = same_document(query_starts, key_starts)
    scores = (
        jnp.einsum("sqhd,skhd->sqhk", queries, key_block, preferred_element_type=jnp.float32)
        * scaling
    )
    weights_f = jnp.where(same_doc, jnp.exp(scores - log_total[..., None]), 0.0)
    grad_weights = jnp.einsum(
        "sqhd,skhd->sqhk", grad_split, value_block, preferred_element_type=jnp.float32
    )
    grad_scores = (weights_f * (grad_weights - row_dot[..., None])).astype(jnp.bfloat16)
    grad_query = (
        jnp.einsum("sqhk,skhd->sqhd", grad_scores, key_block, preferred_element_type=jnp.float32)
        * scaling
    )
    grad_key = (
        jnp.einsum("sqhk,sqhd->skhd", grad_scores, queries, preferred_element_type=jnp.float32)
        * scaling
    )
    grad_value = jnp.einsum(
        "sqhk,sqhd->skhd",
        weights_f.astype(jnp.bfloat16),
        grad_split,
        preferred_element_type=jnp.float32,
    )
    return (grad_query, grad_key, grad_value)


def local(tokens, positions, w_qkv, w_out, w_in, w_down, gain_attn, gain_mlp, cotangent):
    seq_count = tokens.shape[0]
    row_count = tokens.shape[1]
    scaling = HEAD ** (-0.5)
    split_shape = (seq_count, row_count, HEADS, HEAD)
    flat_shape = (seq_count, row_count, D)
    (
        forward_query_weight,
        forward_out_weight,
        forward_in_weight,
        forward_down_weight,
        full_ga,
        full_gm,
    ) = (
        lax.all_gather(w_qkv, ("seq", "wsh"), axis=0, tiled=True),
        lax.all_gather(w_out, ("seq", "wsh"), axis=0, tiled=True),
        lax.all_gather(w_in, ("seq", "wsh"), axis=0, tiled=True),
        lax.all_gather(w_down, ("seq", "wsh"), axis=0, tiled=True),
        lax.all_gather(gain_attn, ("seq", "wsh"), axis=0, tiled=True),
        lax.all_gather(gain_mlp, ("seq", "wsh"), axis=0, tiled=True),
    )
    cosine, sine_table = rotary_tables(positions)
    token_index = lax.axis_index("ctx") * row_count + jnp.arange(row_count, dtype=jnp.int32)
    own_starts = token_index[None, :] - positions
    input_widened = tokens.astype(jnp.float32)
    gain_one = full_ga.astype(jnp.float32)
    gain_two = full_gm.astype(jnp.float32)
    attention_normed = normalize(input_widened, gain_one).astype(jnp.bfloat16)
    projected_output = jnp.einsum(
        "kch,hf->kcf", attention_normed, forward_query_weight, preferred_element_type=jnp.float32
    )
    queries = rotate(projected_output[..., :D].reshape(split_shape), cosine, sine_table).astype(
        jnp.bfloat16
    )
    key_rows = (
        rotate(projected_output[..., D : 2 * D].reshape(split_shape), cosine, sine_table)
        .astype(jnp.bfloat16)
        .reshape(flat_shape)
    )
    value_rows = projected_output[..., 2 * D :].astype(jnp.bfloat16)
    start_state = (
        jnp.full((seq_count, row_count, HEADS), far_below, jnp.float32),
        jnp.zeros((seq_count, row_count, HEADS), jnp.float32),
        jnp.zeros(split_shape, jnp.float32),
    )
    best_score, totals, weighted = fold_keys(
        queries,
        own_starts,
        scaling,
        start_state,
        (
            lax.all_gather(key_rows, "ctx", axis=1, tiled=True),
            lax.all_gather(value_rows, "ctx", axis=1, tiled=True),
            lax.all_gather(own_starts, "ctx", axis=1, tiled=True),
        ),
    )
    attended = weighted / totals[..., None]
    log_total = best_score + jnp.log(totals)
    attended_reduced = attended.reshape(flat_shape).astype(jnp.bfloat16)
    mixed_token_rows = input_widened + jnp.einsum(
        "kch,hf->kcf", attended_reduced, forward_out_weight, preferred_element_type=jnp.float32
    )
    feedforward_normed = normalize(mixed_token_rows, gain_two).astype(jnp.bfloat16)
    hidden_state = jnp.einsum(
        "rnk,kx->rnx", feedforward_normed, forward_in_weight, preferred_element_type=jnp.float32
    )
    inner_part = hidden_state[..., :FF]
    gate_part = hidden_state[..., FF:]
    gated_product = geglu(inner_part, gate_part).astype(jnp.bfloat16)
    output = (
        mixed_token_rows
        + jnp.einsum(
            "ogw,wn->ogn", gated_product, forward_down_weight, preferred_element_type=jnp.float32
        )
    ).astype(jnp.bfloat16)
    backward_query_weight, backward_out_weight, backward_in_weight, backward_down_weight = (
        forward_query_weight,
        forward_out_weight,
        forward_in_weight,
        forward_down_weight,
    )
    down_weight_gradient = jnp.einsum(
        "xvt,xvw->tw", gated_product, cotangent, preferred_element_type=jnp.float32
    )
    grad_product = jnp.einsum(
        "xzi,mi->xzm", cotangent, backward_down_weight, preferred_element_type=jnp.float32
    )
    geglu_pull = jax.vjp(geglu, inner_part, gate_part)[1]
    grad_inner, grad_gate = geglu_pull(grad_product)
    hidden_gradient = jnp.concatenate([grad_inner, grad_gate], -1).astype(jnp.bfloat16)
    grad_w_in = jnp.einsum(
        "hrq,hrw->qw", feedforward_normed, hidden_gradient, preferred_element_type=jnp.float32
    )
    grad_normed_mlp = jnp.einsum(
        "xcu,au->xca", hidden_gradient, backward_in_weight, preferred_element_type=jnp.float32
    )
    mlp_pull = jax.vjp(normalize, mixed_token_rows, gain_two)[1]
    grad_mixed_norm, grad_gain_mlp = mlp_pull(grad_normed_mlp)
    grad_mixed = cotangent.astype(jnp.float32) + grad_mixed_norm
    branch_gradient = grad_mixed.astype(jnp.bfloat16)
    grad_w_out = jnp.einsum(
        "pgj,pgv->jv", attended_reduced, branch_gradient, preferred_element_type=jnp.float32
    )
    grad_attended = jnp.einsum(
        "arq,xq->arx", branch_gradient, backward_out_weight, preferred_element_type=jnp.float32
    ).astype(jnp.bfloat16)
    grad_split = grad_attended.reshape(split_shape)
    row_dot = jnp.sum(grad_split.astype(jnp.float32) * attended, -1)
    cycle_turns = lax.axis_size("ctx") - 1
    zeros_flat = jnp.zeros(flat_shape, jnp.float32)

    def key_turn(turn_index, carried):
        moving_keys, moving_values, moving_starts, grad_keys, grad_values, grad_queries = carried
        grad_query, grad_key, grad_value = block_grads(
            queries,
            own_starts,
            moving_keys.reshape(split_shape),
            moving_values.reshape(split_shape),
            moving_starts,
            grad_split,
            log_total,
            row_dot,
            scaling,
        )
        moving_keys, moving_values, moving_starts = from_behind(
            (moving_keys, moving_values, moving_starts), "ctx", 1
        )
        grad_keys, grad_values = (
            from_behind(
                (grad_keys + grad_key.reshape(flat_shape)).astype(jnp.bfloat16), "ctx", 1
            ).astype(jnp.float32),
            from_behind(
                (grad_values + grad_value.reshape(flat_shape)).astype(jnp.bfloat16), "ctx", 1
            ).astype(jnp.float32),
        )
        return (
            moving_keys,
            moving_values,
            moving_starts,
            grad_keys,
            grad_values,
            grad_queries + grad_query,
        )

    moving_keys, moving_values, moving_starts, grad_keys, grad_values, grad_queries = lax.fori_loop(
        0,
        cycle_turns,
        key_turn,
        (
            key_rows,
            value_rows,
            own_starts,
            zeros_flat,
            zeros_flat,
            jnp.zeros(split_shape, jnp.float32),
        ),
    )
    grad_query, grad_key, grad_value = block_grads(
        queries,
        own_starts,
        moving_keys.reshape(split_shape),
        moving_values.reshape(split_shape),
        moving_starts,
        grad_split,
        log_total,
        row_dot,
        scaling,
    )
    grad_queries = grad_queries + grad_query
    grad_keys, grad_values = (
        from_behind(
            (grad_keys + grad_key.reshape(flat_shape)).astype(jnp.bfloat16), "ctx", 1
        ).astype(jnp.float32),
        from_behind(
            (grad_values + grad_value.reshape(flat_shape)).astype(jnp.bfloat16), "ctx", 1
        ).astype(jnp.float32),
    )
    projected_gradient = jnp.concatenate(
        [
            rotate_back(grad_queries, cosine, sine_table).reshape(flat_shape),
            rotate_back(grad_keys.reshape(split_shape), cosine, sine_table).reshape(flat_shape),
            grad_values,
        ],
        -1,
    ).astype(jnp.bfloat16)
    grad_w_qkv = jnp.einsum(
        "pgj,pgv->jv", attention_normed, projected_gradient, preferred_element_type=jnp.float32
    )
    grad_normed_attn = jnp.einsum(
        "arq,xq->arx", projected_gradient, backward_query_weight, preferred_element_type=jnp.float32
    )
    attn_pull = jax.vjp(normalize, input_widened, gain_one)[1]
    grad_inputs_norm, grad_gain_attn = attn_pull(grad_normed_attn)
    grad_tokens = (grad_mixed + grad_inputs_norm).astype(jnp.bfloat16)
    shares = (
        lax.psum_scatter(
            grad_w_qkv.astype(jnp.bfloat16), ("seq", "wsh"), scatter_dimension=0, tiled=True
        ).astype(jnp.float32),
        lax.psum_scatter(
            grad_w_out.astype(jnp.bfloat16), ("seq", "wsh"), scatter_dimension=0, tiled=True
        ).astype(jnp.float32),
        lax.psum_scatter(
            grad_w_in.astype(jnp.bfloat16), ("seq", "wsh"), scatter_dimension=0, tiled=True
        ).astype(jnp.float32),
        lax.psum_scatter(
            down_weight_gradient.astype(jnp.bfloat16),
            ("seq", "wsh"),
            scatter_dimension=0,
            tiled=True,
        ).astype(jnp.float32),
        lax.psum_scatter(
            grad_gain_attn.astype(jnp.bfloat16), ("seq", "wsh"), scatter_dimension=0, tiled=True
        ).astype(jnp.float32),
        lax.psum_scatter(
            grad_gain_mlp.astype(jnp.bfloat16), ("seq", "wsh"), scatter_dimension=0, tiled=True
        ).astype(jnp.float32),
    )
    summed = lax.psum((shares[0], shares[1], shares[2], shares[3], shares[4], shares[5]), "ctx")
    return (output, grad_tokens, summed[0], summed[1], summed[2], summed[3], summed[4], summed[5])


GROUP = ("seq", "wsh")
MESH = pl.DeviceIdType.MESH


def group_peer(index):
    return {"seq": index // 2, "wsh": lax.rem(index, 2)}


def ctx_peer(index):
    return {"ctx": index}


def exchange_kernel(size, group, spread, src, dst, send_sems, recv_sems, own_sem):
    if group:
        me = lax.axis_index("seq") * 2 + lax.axis_index("wsh")
        peer_of = group_peer
    else:
        me = lax.axis_index("ctx")
        peer_of = ctx_peer
    barrier = pltpu.get_barrier_semaphore()
    for step in range(1, size):
        pl.semaphore_signal(
            barrier, inc=1, device_id=peer_of(lax.rem(me + step, size)), device_id_type=MESH
        )
    pl.semaphore_wait(barrier, size - 1)
    copies = []
    for step in range(1, size):
        peer = lax.rem(me + step, size)
        copy = pltpu.make_async_remote_copy(
            src_ref=src.at[peer] if spread else src,
            dst_ref=dst.at[me],
            send_sem=send_sems.at[step - 1],
            recv_sem=recv_sems.at[step - 1],
            device_id=peer_of(peer),
            device_id_type=MESH,
        )
        copy.start()
        copies.append(copy)
    own = pltpu.make_async_copy(src.at[me] if spread else src, dst.at[me], own_sem)
    own.start()
    own.wait()
    for copy in copies:
        copy.wait()


def exchange(shard, size, group, spread, number):
    shape = shard.shape if spread else (size,) + shard.shape
    return pl.pallas_call(
        functools.partial(exchange_kernel, size, group, spread),
        out_shape=jax.ShapeDtypeStruct(shape, shard.dtype),
        in_specs=[pl.BlockSpec(memory_space=pl.ANY)],
        out_specs=pl.BlockSpec(memory_space=pl.ANY),
        scratch_shapes=[
            pltpu.SemaphoreType.DMA((size - 1,)),
            pltpu.SemaphoreType.DMA((size - 1,)),
            pltpu.SemaphoreType.DMA,
        ],
        compiler_params=pltpu.CompilerParams(collective_id=number, has_side_effects=True),
    )(shard)


def reduce_kernel(turns, size, count, *refs):
    low, wide = jnp.bfloat16, jnp.float32
    grads, outs = refs[:count], refs[count : 2 * count]
    from_y, from_z, total = (refs[(2 + i) * count : (3 + i) * count] for i in range(3))
    sends, recvs = refs[5 * count : 5 * count + 2]
    depth = size // 2
    parts = 4
    me = lax.axis_index("ctx")
    place, side = me // 2, lax.rem(me, 2)
    across = me + 1 - 2 * side
    group_me = lax.axis_index("seq") * 2 + lax.axis_index("wsh")
    z_peers = [lax.rem(place + step, depth) for step in range(1, depth)]
    x_peers = [lax.rem(group_me + step, parts) for step in range(1, parts)]

    barrier = pltpu.get_barrier_semaphore()
    pl.semaphore_signal(barrier, inc=1, device_id=ctx_peer(across), device_id_type=MESH)
    for peer in z_peers:
        pl.semaphore_signal(
            barrier, inc=1, device_id=ctx_peer(peer * 2 + side), device_id_type=MESH
        )
    for peer in x_peers:
        pl.semaphore_signal(barrier, inc=1, device_id=group_peer(peer), device_id_type=MESH)
    pl.semaphore_wait(barrier, 1 + len(z_peers) + len(x_peers))

    def remote(chunk, slot, source, target, device):
        copy = pltpu.make_async_remote_copy(
            src_ref=source,
            dst_ref=target,
            send_sem=sends.at[chunk, slot],
            recv_sem=recvs.at[chunk, slot],
            device_id=device,
            device_id_type=MESH,
        )
        copy.start()
        return copy

    def by_rows(rows, step_body):
        block = 32 if rows % 32 == 0 else 16

        def body(index, carry):
            step_body(pl.ds(pl.multiple_of(index * block, block), block))
            return carry

        lax.fori_loop(0, rows // block, body, 0)

    z_slot = depth
    x_slot = z_slot + depth - 1
    zg_slot = x_slot + parts - 1
    yg_slot = zg_slot + depth - 1
    ys, zs, xs, zgs, ygs = ({} for _ in range(5))

    def start_y(c):
        ys[c] = [
            remote(c, z, grads[c].at[2 * z + 1 - side], from_y[c].at[z], ctx_peer(across))
            for z in range(depth)
        ]

    def start_z(c):
        rows = total[c].shape[0]
        for copy in ys[c]:
            copy.wait()

        def add(at):
            for z in range(depth):
                from_y[c][z, at, :] = (
                    grads[c][2 * z + side, at, :].astype(wide) + from_y[c][z, at, :].astype(wide)
                ).astype(low)

        by_rows(rows, add)
        zs[c] = [
            remote(
                c, z_slot + i, from_y[c].at[peer], from_z[c].at[place], ctx_peer(peer * 2 + side)
            )
            for i, peer in enumerate(z_peers)
        ]

    def start_x(c):
        rows = total[c].shape[0]
        for copy in zs[c]:
            copy.wait()

        def add(at):
            summed = from_y[c][place, at, :].astype(wide)
            for peer in z_peers:
                summed = summed + from_z[c][peer, at, :].astype(wide)
            if turns[c]:
                total[c][at, :] = summed.astype(low)
            else:
                outs[c][me, at, :] = summed.astype(low)

        by_rows(rows, add)
        if turns[c]:
            piece = rows // parts
            xs[c] = [
                remote(
                    c,
                    x_slot + i,
                    total[c].at[pl.ds(pl.multiple_of(peer * piece, piece), piece)],
                    outs[c].at[me, pl.ds(pl.multiple_of(group_me * piece, piece), piece)],
                    group_peer(peer),
                )
                for i, peer in enumerate(x_peers)
            ]
            mine = pl.ds(pl.multiple_of(group_me * piece, piece), piece)
            outs[c][me, mine, :] = total[c][mine, :]

    def start_zg(c):
        if turns[c]:
            for copy in xs[c]:
                copy.wait()
        zgs[c] = [
            remote(c, zg_slot + i, outs[c].at[me], outs[c].at[me], ctx_peer(peer * 2 + side))
            for i, peer in enumerate(z_peers)
        ]
        ygs[c] = [remote(c, yg_slot, outs[c].at[me], outs[c].at[me], ctx_peer(across))]

    def start_yg(c):
        for i, (copy, step) in enumerate(zip(zgs[c], range(1, depth))):
            copy.wait()
            came = lax.rem(place + depth - step, depth) * 2 + side
            ygs[c].append(
                remote(c, yg_slot + step, outs[c].at[came], outs[c].at[came], ctx_peer(across))
            )

    for c in range(count):
        start_y(c)
    for turn in range(count + 3):
        for stage, back in ((start_z, 0), (start_x, 1), (start_zg, 2), (start_yg, 3)):
            if 0 <= turn - back < count:
                stage(turn - back)
    for c in range(count):
        for copy in ygs[c]:
            copy.wait()


def reduce_over_ctx(grads, turns, size, number):
    count = len(grads)
    depth = size // 2
    slots = depth + 2 * (depth - 1) + 3 + depth
    whole = pl.BlockSpec(memory_space=pltpu.VMEM)
    pairs = [pltpu.VMEM((depth,) + g.shape[1:], g.dtype) for g in grads]
    totals = [pltpu.VMEM(g.shape[1:], g.dtype) for g in grads]
    return pl.pallas_call(
        functools.partial(reduce_kernel, turns, size, count),
        out_shape=[jax.ShapeDtypeStruct(g.shape, g.dtype) for g in grads],
        in_specs=[whole] * count,
        out_specs=[whole] * count,
        scratch_shapes=pairs
        + pairs
        + totals
        + [pltpu.SemaphoreType.DMA((count, slots)), pltpu.SemaphoreType.DMA((count, slots))],
        compiler_params=pltpu.CompilerParams(
            collective_id=number, has_side_effects=True, vmem_limit_bytes=48 * 1024 * 1024
        ),
    )(*grads)


def permute_group(chunk_for, parts):
    me = lax.axis_index(GROUP)
    came = [chunk_for(me)]
    for step in range(1, parts):
        pairs = [(i, i ^ step) for i in range(parts)]
        came.append(lax.ppermute(chunk_for(me ^ step), GROUP, pairs))
    order = jnp.arange(parts) ^ me
    return jnp.stack(came)[order]


def layer_norm_parts(values):
    middle = jnp.mean(values, -1, keepdims=True)
    centred = values - middle
    factor = lax.rsqrt(jnp.mean(centred * centred, -1, keepdims=True) + layer_eps)
    return centred * factor, factor


def norm_back(grad, gain, normed, factor):
    scaled = grad * gain
    return factor * (
        scaled
        - jnp.mean(scaled, -1, keepdims=True)
        - normed * jnp.mean(scaled * normed, -1, keepdims=True)
    )


def dot(equation, left, right):
    return jnp.einsum(equation, left, right, preferred_element_type=jnp.float32)


def parallel(parts, ctx_size, tokens, positions, w_qkv, w_out, w_in, w_down, gain_attn, gain_mlp,
             cotangent):
    low = jnp.bfloat16
    wide = jnp.float32
    row_count = tokens.shape[1]
    length = row_count * ctx_size
    part_heads = HEADS // parts
    part_ff = FF // parts
    part_d = D // parts
    pairs = parts * part_heads // ctx_size
    seq_split = part_heads // pairs
    half = HEAD // 2
    scaling = HEAD ** (-0.5)
    ctx_index = lax.axis_index("ctx")

    def gather(shard, number):
        return exchange(shard, parts, True, False, number)

    def swap(shard, number):
        return exchange(shard, parts, True, True, number)

    def swap_ctx(shard, number):
        return exchange(shard, ctx_size, False, True, number)

    def gather_ctx(shard, number):
        return exchange(shard, ctx_size, False, False, number)

    inputs = tokens[0].astype(wide)
    cot = cotangent[0]
    small = jnp.concatenate(
        [positions[0].astype(wide), gain_attn.astype(wide), gain_mlp.astype(wide)]
    )
    small = gather(small.reshape(-1, 128), 25).reshape(parts, -1)
    gain_one = small[:, row_count : row_count + part_d].reshape(D)
    gain_two = small[:, row_count + part_d :].reshape(D)
    all_positions = (
        gather_ctx(small[:, :row_count].astype(jnp.int32), 26).transpose(1, 0, 2).reshape(parts, length)
    )
    starts = jnp.arange(length, dtype=jnp.int32)[None, :] - all_positions
    group_positions = lax.dynamic_slice_in_dim(all_positions, ctx_index * row_count, row_count, 1)
    my_seq = ctx_index // seq_split
    seq_positions = lax.dynamic_index_in_dim(all_positions, my_seq, 0, False)
    seq_starts = lax.dynamic_index_in_dim(starts, my_seq, 0, False)

    in_split = w_in.reshape(part_d, 2, parts, part_ff)
    in_cols = permute_group(
        lambda peer: lax.dynamic_index_in_dim(in_split, peer, 2, False), parts
    ).reshape(D, 2 * part_ff)
    all_cot = permute_group(lambda peer: cot, parts)
    qkv_cols = swap(
        w_qkv.reshape(part_d, 3, parts, part_d).transpose(2, 0, 1, 3).reshape(parts, part_d, 3 * part_d),
        1,
    ).reshape(D, 3 * part_d)
    norm_one, factor_one = layer_norm_parts(inputs)
    normed_attn = gather((norm_one * gain_one).astype(low), 2)
    projected = dot("stc,cf->stf", normed_attn, qkv_cols)
    cosine, sine = rotary_tables(group_positions)
    turned = [
        rotate(
            projected[..., i * part_d : (i + 1) * part_d].reshape(
                parts, row_count, part_heads, HEAD
            ),
            cosine,
            sine,
        )
        for i in range(2)
    ]
    turned.append(projected[..., 2 * part_d :].reshape(parts, row_count, part_heads, HEAD))
    heads_out = jnp.stack([t.astype(low) for t in turned])
    heads_out = (
        heads_out.reshape(3, parts, row_count, seq_split, pairs * HEAD)
        .transpose(1, 3, 2, 0, 4)
        .reshape(ctx_size, row_count, 3 * pairs * HEAD)
    )
    heads_in = swap_ctx(heads_out, 3).reshape(length, 3, pairs, HEAD).transpose(1, 2, 0, 3)
    queries, keys, values = heads_in
    same = (seq_starts[:, None] == seq_starts[None, :])[None]
    scores = jnp.where(same, dot("hqd,hkd->hqk", queries, keys) * scaling, far_below)
    best = jnp.max(scores, -1, keepdims=True)
    raised = jnp.where(same, jnp.exp(scores - best), 0.0)
    totals = jnp.sum(raised, -1, keepdims=True)
    log_total = best + jnp.log(totals)
    attended = dot("hqk,hkd->hqd", raised.astype(low), values) / totals

    def to_tokens(shard, width):
        return (
            shard.transpose(1, 0, 2).reshape(ctx_size, row_count, pairs * width)
        )

    def from_ctx(shard):
        return (
            shard.reshape(parts, seq_split, row_count, -1)
            .transpose(0, 2, 1, 3)
            .reshape(parts, row_count, -1)
        )

    attended_low = from_ctx(swap_ctx(to_tokens(attended.astype(low), HEAD), 4))
    branch = swap(dot("stc,cf->stf", attended_low, w_out).astype(low), 5)
    mixed = inputs + jnp.sum(branch.astype(wide), 0)
    norm_two, factor_two = layer_norm_parts(mixed)
    normed_mlp = gather((norm_two * gain_two).astype(low), 6)
    hidden = dot("stc,cf->stf", normed_mlp, in_cols)
    inner, gate = hidden[..., :part_ff], hidden[..., part_ff:]
    product, pull = jax.vjp(geglu, inner, gate)
    product = product.astype(low)
    grad_product = dot("stn,fn->stf", all_cot, w_down)
    grad_inner, grad_gate = pull(grad_product)
    grad_hidden = jnp.concatenate([grad_inner, grad_gate], -1).astype(low)
    normed_back = swap(dot("stf,cf->stc", grad_hidden, in_cols).astype(low), 9)
    grad_normed_mlp = jnp.sum(normed_back.astype(wide), 0)
    grad_gain_mlp = jnp.sum(grad_normed_mlp * norm_two, 0)
    grad_mixed = cot.astype(wide) + norm_back(grad_normed_mlp, gain_two, norm_two, factor_two)
    grad_branch = gather(grad_mixed.astype(low), 10)
    grad_attended = dot("stf,cf->stc", grad_branch, w_out).astype(low)
    grad_out = (
        grad_attended.reshape(parts, row_count, seq_split, pairs * HEAD)
        .transpose(0, 2, 1, 3)
        .reshape(ctx_size, row_count, pairs * HEAD)
    )
    grad_heads = swap_ctx(grad_out, 11).reshape(length, pairs, HEAD).transpose(1, 0, 2)

    output_parts = swap(dot("stf,fn->stn", product, w_down).astype(low), 12)
    output = (mixed + jnp.sum(output_parts.astype(wide), 0)).astype(low)

    def rows_of(grad, width):
        return (
            grad.reshape(parts, ctx_size, part_d // ctx_size, width)
            .transpose(1, 0, 2, 3)
            .reshape(ctx_size, -1, width)
            .astype(low)
        )

    def columns_of(grad):
        rows = grad.shape[0]
        return grad.reshape(rows, ctx_size, D // ctx_size).transpose(1, 0, 2).astype(low)

    def back_to_rows(grad, pieces):
        width = grad.shape[-1] // pieces
        return (
            grad.reshape(ctx_size, parts, part_d // ctx_size, pieces, width)
            .transpose(0, 2, 3, 1, 4)
            .reshape(part_d, -1)
            .astype(wide)
        )

    def back_to_columns(grad):
        return grad.transpose(1, 0, 2).reshape(grad.shape[1], D).astype(wide)

    down_grad = columns_of(dot("stf,stn->fn", product, all_cot))
    in_grad = rows_of(dot("stc,stf->cf", normed_mlp, grad_hidden), 2 * part_ff)

    row_dot = jnp.sum(grad_heads.astype(wide) * attended, -1, keepdims=True)
    weights_f = jnp.where(same, jnp.exp(scores - log_total), 0.0)
    grad_weights = dot("hqd,hkd->hqk", grad_heads, values)
    grad_scores = (weights_f * (grad_weights - row_dot)).astype(low)
    grad_queries = dot("hqk,hkd->hqd", grad_scores, keys) * scaling
    grad_keys = dot("hqk,hqd->hkd", grad_scores, queries) * scaling
    grad_values = dot("hqk,hqd->hkd", weights_f.astype(low), grad_heads)
    seq_cos, seq_sin = rotary_tables(seq_positions)
    seq_cos, seq_sin = seq_cos[:, 0][None], seq_sin[:, 0][None]
    grads = jnp.stack(
        [
            rotate_back(grad_queries, seq_cos, seq_sin),
            rotate_back(grad_keys, seq_cos, seq_sin),
            grad_values,
        ]
    ).astype(low)
    grads = grads.transpose(2, 0, 1, 3).reshape(ctx_size, row_count, 3 * pairs * HEAD)
    grads = swap_ctx(grads, 15)
    grad_projected = (
        grads.reshape(parts, seq_split, row_count, 3, pairs * HEAD)
        .transpose(0, 2, 3, 1, 4)
        .reshape(parts, row_count, 3 * part_d)
    )
    attn_back = swap(dot("stf,cf->stc", grad_projected, qkv_cols).astype(low), 16)
    grad_normed_attn = jnp.sum(attn_back.astype(wide), 0)
    grad_gain_attn = jnp.sum(grad_normed_attn * norm_one, 0)
    grad_tokens = (
        grad_mixed + norm_back(grad_normed_attn, gain_one, norm_one, factor_one)
    ).astype(low)

    out_grad = columns_of(dot("stc,stf->cf", attended_low, grad_branch))
    qkv_grad = rows_of(dot("stc,stf->cf", normed_attn, grad_projected), 3 * part_d)
    out_grad, down_grad, qkv_grad, in_grad = reduce_over_ctx(
        [out_grad, down_grad, qkv_grad, in_grad], (False, False, True, True), ctx_size, 13
    )
    gain_sums = jnp.stack([grad_gain_attn, grad_gain_mlp]).reshape(2, parts, part_d)
    gain_sums = jnp.sum(swap(gain_sums.transpose(1, 0, 2), 27), 0)
    gain_sums = jnp.sum(gather_ctx(gain_sums, 28), 0)
    return (
        output[None],
        grad_tokens[None],
        back_to_rows(qkv_grad, 3),
        back_to_columns(out_grad),
        back_to_rows(in_grad, 2),
        back_to_columns(down_grad),
        gain_sums[0],
        gain_sums[1],
    )


def solution(mesh):
    placed = (
        P(("seq", "wsh"), "ctx", None),
        P(("seq", "wsh"), "ctx"),
        P(("seq", "wsh"), None),
        P(("seq", "wsh"), None),
        P(("seq", "wsh"), None),
        P(("seq", "wsh"), None),
        P(("seq", "wsh")),
        P(("seq", "wsh")),
        P(("seq", "wsh"), "ctx", None),
    )
    parts = mesh.shape["seq"] * mesh.shape["wsh"]
    ctx_size = mesh.shape["ctx"]
    whole_pairs = HEADS % ctx_size == 0 and ctx_size % 2 == 0 and parts == 4
    body = functools.partial(parallel, parts, ctx_size) if whole_pairs else local
    return jax.shard_map(
        body,
        mesh=mesh,
        in_specs=placed,
        out_specs=(
            P(("seq", "wsh"), "ctx", None),
            P(("seq", "wsh"), "ctx", None),
            P(("seq", "wsh"), None),
            P(("seq", "wsh"), None),
            P(("seq", "wsh"), None),
            P(("seq", "wsh"), None),
            P(("seq", "wsh")),
            P(("seq", "wsh")),
        ),
        check_vma=False,
    )
```

```python
import functools
import math

import jax
import jax.numpy as jnp
from jax import lax
from jax.experimental import pallas as pl
from jax.experimental.pallas import tpu as pltpu
from jax.sharding import PartitionSpec as P

D = 1024
HEADS = 16
HEAD = 64
FF = 2624


layer_eps = 1e-05
rope_base = 160000.0
far_below = -1e30


def from_behind(shard, axis, by):
    size = lax.axis_size(axis)
    return lax.ppermute(shard, axis, [(i, (i + by) % size) for i in range(size)])


def normalize(values, gain_vector):
    middle = jnp.mean(values, -1, keepdims=True)
    centred = values - middle
    spread = jnp.mean(centred * centred, -1, keepdims=True)
    return centred * lax.rsqrt(spread + layer_eps) * gain_vector


def rotary_tables(positions):
    half_size = HEAD // 2
    frequency = jnp.exp(
        jnp.arange(half_size, dtype=jnp.float32) * (-2.0 * math.log(rope_base) / HEAD)
    )
    angles = positions.astype(jnp.float32)[..., None] * frequency
    cosine = jnp.cos(angles)
    sine_table = jnp.sin(angles)
    return (
        jnp.concatenate([cosine, cosine], -1)[..., None, :],
        jnp.concatenate([sine_table, sine_table], -1)[..., None, :],
    )


def rotate(values, cosine, sine_table):
    half_size = values.shape[-1] // 2
    turned = jnp.concatenate([-values[..., half_size:], values[..., :half_size]], -1)
    return values * cosine + turned * sine_table


def rotate_back(grads, cosine, sine_table):
    half_size = grads.shape[-1] // 2
    shifted = grads * sine_table
    return grads * cosine + jnp.concatenate(
        [shifted[..., half_size:], -shifted[..., :half_size]], -1
    )


def geglu(inner_part, gate_part):
    return jax.nn.gelu(inner_part, approximate=False) * gate_part


def same_document(query_starts, key_starts):
    return (query_starts[:, :, None] == key_starts[:, None, :])[:, :, None, :]


def fold_keys(queries, query_starts, scaling, running, piece):
    key_piece, value_piece, start_piece = piece
    seq_count = key_piece.shape[0]
    row_total = key_piece.shape[1]
    block_size = math.gcd(row_total, 512)

    def one_block(block_index, carried):
        best_score, totals, weighted = carried
        key_block = lax.dynamic_slice_in_dim(
            key_piece, block_index * block_size, block_size, 1
        ).reshape(seq_count, block_size, HEADS, HEAD)
        value_block = lax.dynamic_slice_in_dim(
            value_piece, block_index * block_size, block_size, 1
        ).reshape(seq_count, block_size, HEADS, HEAD)
        start_block = lax.dynamic_slice_in_dim(start_piece, block_index * block_size, block_size, 1)
        same_doc = same_document(query_starts, start_block)
        scores = (
            jnp.einsum("sqhd,skhd->sqhk", queries, key_block, preferred_element_type=jnp.float32)
            * scaling
        )
        scores = jnp.where(same_doc, scores, far_below)
        new_best = jnp.maximum(best_score, jnp.max(scores, -1))
        fading = jnp.exp(best_score - new_best)
        raised = jnp.where(same_doc, jnp.exp(scores - new_best[..., None]), 0.0)
        totals = totals * fading + jnp.sum(raised, -1)
        weighted = weighted * fading[..., None] + jnp.einsum(
            "sqhk,skhd->sqhd",
            raised.astype(jnp.bfloat16),
            value_block,
            preferred_element_type=jnp.float32,
        )
        return (new_best, totals, weighted)

    return lax.fori_loop(0, row_total // block_size, one_block, running)


def block_grads(
    queries,
    query_starts,
    key_block,
    value_block,
    key_starts,
    grad_split,
    log_total,
    row_dot,
    scaling,
):
    same_doc = same_document(query_starts, key_starts)
    scores = (
        jnp.einsum("sqhd,skhd->sqhk", queries, key_block, preferred_element_type=jnp.float32)
        * scaling
    )
    weights_f = jnp.where(same_doc, jnp.exp(scores - log_total[..., None]), 0.0)
    grad_weights = jnp.einsum(
        "sqhd,skhd->sqhk", grad_split, value_block, preferred_element_type=jnp.float32
    )
    grad_scores = (weights_f * (grad_weights - row_dot[..., None])).astype(jnp.bfloat16)
    grad_query = (
        jnp.einsum("sqhk,skhd->sqhd", grad_scores, key_block, preferred_element_type=jnp.float32)
        * scaling
    )
    grad_key = (
        jnp.einsum("sqhk,sqhd->skhd", grad_scores, queries, preferred_element_type=jnp.float32)
        * scaling
    )
    grad_value = jnp.einsum(
        "sqhk,sqhd->skhd",
        weights_f.astype(jnp.bfloat16),
        grad_split,
        preferred_element_type=jnp.float32,
    )
    return (grad_query, grad_key, grad_value)


def local(tokens, positions, w_qkv, w_out, w_in, w_down, gain_attn, gain_mlp, cotangent):
    seq_count = tokens.shape[0]
    row_count = tokens.shape[1]
    scaling = HEAD ** (-0.5)
    split_shape = (seq_count, row_count, HEADS, HEAD)
    flat_shape = (seq_count, row_count, D)
    (
        forward_query_weight,
        forward_out_weight,
        forward_in_weight,
        forward_down_weight,
        full_ga,
        full_gm,
    ) = (
        lax.all_gather(w_qkv, ("seq", "wsh"), axis=0, tiled=True),
        lax.all_gather(w_out, ("seq", "wsh"), axis=0, tiled=True),
        lax.all_gather(w_in, ("seq", "wsh"), axis=0, tiled=True),
        lax.all_gather(w_down, ("seq", "wsh"), axis=0, tiled=True),
        lax.all_gather(gain_attn, ("seq", "wsh"), axis=0, tiled=True),
        lax.all_gather(gain_mlp, ("seq", "wsh"), axis=0, tiled=True),
    )
    cosine, sine_table = rotary_tables(positions)
    token_index = lax.axis_index("ctx") * row_count + jnp.arange(row_count, dtype=jnp.int32)
    own_starts = token_index[None, :] - positions
    input_widened = tokens.astype(jnp.float32)
    gain_one = full_ga.astype(jnp.float32)
    gain_two = full_gm.astype(jnp.float32)
    attention_normed = normalize(input_widened, gain_one).astype(jnp.bfloat16)
    projected_output = jnp.einsum(
        "kch,hf->kcf", attention_normed, forward_query_weight, preferred_element_type=jnp.float32
    )
    queries = rotate(projected_output[..., :D].reshape(split_shape), cosine, sine_table).astype(
        jnp.bfloat16
    )
    key_rows = (
        rotate(projected_output[..., D : 2 * D].reshape(split_shape), cosine, sine_table)
        .astype(jnp.bfloat16)
        .reshape(flat_shape)
    )
    value_rows = projected_output[..., 2 * D :].astype(jnp.bfloat16)
    start_state = (
        jnp.full((seq_count, row_count, HEADS), far_below, jnp.float32),
        jnp.zeros((seq_count, row_count, HEADS), jnp.float32),
        jnp.zeros(split_shape, jnp.float32),
    )
    best_score, totals, weighted = fold_keys(
        queries,
        own_starts,
        scaling,
        start_state,
        (
            lax.all_gather(key_rows, "ctx", axis=1, tiled=True),
            lax.all_gather(value_rows, "ctx", axis=1, tiled=True),
            lax.all_gather(own_starts, "ctx", axis=1, tiled=True),
        ),
    )
    attended = weighted / totals[..., None]
    log_total = best_score + jnp.log(totals)
    attended_reduced = attended.reshape(flat_shape).astype(jnp.bfloat16)
    mixed_token_rows = input_widened + jnp.einsum(
        "kch,hf->kcf", attended_reduced, forward_out_weight, preferred_element_type=jnp.float32
    )
    feedforward_normed = normalize(mixed_token_rows, gain_two).astype(jnp.bfloat16)
    hidden_state = jnp.einsum(
        "rnk,kx->rnx", feedforward_normed, forward_in_weight, preferred_element_type=jnp.float32
    )
    inner_part = hidden_state[..., :FF]
    gate_part = hidden_state[..., FF:]
    gated_product = geglu(inner_part, gate_part).astype(jnp.bfloat16)
    output = (
        mixed_token_rows
        + jnp.einsum(
            "ogw,wn->ogn", gated_product, forward_down_weight, preferred_element_type=jnp.float32
        )
    ).astype(jnp.bfloat16)
    backward_query_weight, backward_out_weight, backward_in_weight, backward_down_weight = (
        forward_query_weight,
        forward_out_weight,
        forward_in_weight,
        forward_down_weight,
    )
    down_weight_gradient = jnp.einsum(
        "xvt,xvw->tw", gated_product, cotangent, preferred_element_type=jnp.float32
    )
    grad_product = jnp.einsum(
        "xzi,mi->xzm", cotangent, backward_down_weight, preferred_element_type=jnp.float32
    )
    geglu_pull = jax.vjp(geglu, inner_part, gate_part)[1]
    grad_inner, grad_gate = geglu_pull(grad_product)
    hidden_gradient = jnp.concatenate([grad_inner, grad_gate], -1).astype(jnp.bfloat16)
    grad_w_in = jnp.einsum(
        "hrq,hrw->qw", feedforward_normed, hidden_gradient, preferred_element_type=jnp.float32
    )
    grad_normed_mlp = jnp.einsum(
        "xcu,au->xca", hidden_gradient, backward_in_weight, preferred_element_type=jnp.float32
    )
    mlp_pull = jax.vjp(normalize, mixed_token_rows, gain_two)[1]
    grad_mixed_norm, grad_gain_mlp = mlp_pull(grad_normed_mlp)
    grad_mixed = cotangent.astype(jnp.float32) + grad_mixed_norm
    branch_gradient = grad_mixed.astype(jnp.bfloat16)
    grad_w_out = jnp.einsum(
        "pgj,pgv->jv", attended_reduced, branch_gradient, preferred_element_type=jnp.float32
    )
    grad_attended = jnp.einsum(
        "arq,xq->arx", branch_gradient, backward_out_weight, preferred_element_type=jnp.float32
    ).astype(jnp.bfloat16)
    grad_split = grad_attended.reshape(split_shape)
    row_dot = jnp.sum(grad_split.astype(jnp.float32) * attended, -1)
    cycle_turns = lax.axis_size("ctx") - 1
    zeros_flat = jnp.zeros(flat_shape, jnp.float32)

    def key_turn(turn_index, carried):
        moving_keys, moving_values, moving_starts, grad_keys, grad_values, grad_queries = carried
        grad_query, grad_key, grad_value = block_grads(
            queries,
            own_starts,
            moving_keys.reshape(split_shape),
            moving_values.reshape(split_shape),
            moving_starts,
            grad_split,
            log_total,
            row_dot,
            scaling,
        )
        moving_keys, moving_values, moving_starts = from_behind(
            (moving_keys, moving_values, moving_starts), "ctx", 1
        )
        grad_keys, grad_values = (
            from_behind(
                (grad_keys + grad_key.reshape(flat_shape)).astype(jnp.bfloat16), "ctx", 1
            ).astype(jnp.float32),
            from_behind(
                (grad_values + grad_value.reshape(flat_shape)).astype(jnp.bfloat16), "ctx", 1
            ).astype(jnp.float32),
        )
        return (
            moving_keys,
            moving_values,
            moving_starts,
            grad_keys,
            grad_values,
            grad_queries + grad_query,
        )

    moving_keys, moving_values, moving_starts, grad_keys, grad_values, grad_queries = lax.fori_loop(
        0,
        cycle_turns,
        key_turn,
        (
            key_rows,
            value_rows,
            own_starts,
            zeros_flat,
            zeros_flat,
            jnp.zeros(split_shape, jnp.float32),
        ),
    )
    grad_query, grad_key, grad_value = block_grads(
        queries,
        own_starts,
        moving_keys.reshape(split_shape),
        moving_values.reshape(split_shape),
        moving_starts,
        grad_split,
        log_total,
        row_dot,
        scaling,
    )
    grad_queries = grad_queries + grad_query
    grad_keys, grad_values = (
        from_behind(
            (grad_keys + grad_key.reshape(flat_shape)).astype(jnp.bfloat16), "ctx", 1
        ).astype(jnp.float32),
        from_behind(
            (grad_values + grad_value.reshape(flat_shape)).astype(jnp.bfloat16), "ctx", 1
        ).astype(jnp.float32),
    )
    projected_gradient = jnp.concatenate(
        [
            rotate_back(grad_queries, cosine, sine_table).reshape(flat_shape),
            rotate_back(grad_keys.reshape(split_shape), cosine, sine_table).reshape(flat_shape),
            grad_values,
        ],
        -1,
    ).astype(jnp.bfloat16)
    grad_w_qkv = jnp.einsum(
        "pgj,pgv->jv", attention_normed, projected_gradient, preferred_element_type=jnp.float32
    )
    grad_normed_attn = jnp.einsum(
        "arq,xq->arx", projected_gradient, backward_query_weight, preferred_element_type=jnp.float32
    )
    attn_pull = jax.vjp(normalize, input_widened, gain_one)[1]
    grad_inputs_norm, grad_gain_attn = attn_pull(grad_normed_attn)
    grad_tokens = (grad_mixed + grad_inputs_norm).astype(jnp.bfloat16)
    shares = (
        lax.psum_scatter(
            grad_w_qkv.astype(jnp.bfloat16), ("seq", "wsh"), scatter_dimension=0, tiled=True
        ).astype(jnp.float32),
        lax.psum_scatter(
            grad_w_out.astype(jnp.bfloat16), ("seq", "wsh"), scatter_dimension=0, tiled=True
        ).astype(jnp.float32),
        lax.psum_scatter(
            grad_w_in.astype(jnp.bfloat16), ("seq", "wsh"), scatter_dimension=0, tiled=True
        ).astype(jnp.float32),
        lax.psum_scatter(
            down_weight_gradient.astype(jnp.bfloat16),
            ("seq", "wsh"),
            scatter_dimension=0,
            tiled=True,
        ).astype(jnp.float32),
        lax.psum_scatter(
            grad_gain_attn.astype(jnp.bfloat16), ("seq", "wsh"), scatter_dimension=0, tiled=True
        ).astype(jnp.float32),
        lax.psum_scatter(
            grad_gain_mlp.astype(jnp.bfloat16), ("seq", "wsh"), scatter_dimension=0, tiled=True
        ).astype(jnp.float32),
    )
    summed = lax.psum((shares[0], shares[1], shares[2], shares[3], shares[4], shares[5]), "ctx")
    return (output, grad_tokens, summed[0], summed[1], summed[2], summed[3], summed[4], summed[5])


GROUP = ("seq", "wsh")
MESH = pl.DeviceIdType.MESH


def group_peer(index):
    return {"seq": index // 2, "wsh": lax.rem(index, 2)}


def ctx_peer(index):
    return {"ctx": index}


def exchange_kernel(size, group, spreads, *refs):
    count = len(spreads)
    sources, targets = refs[:count], refs[count : 2 * count]
    send_sems, recv_sems, own_sems = refs[2 * count :]
    if group:
        me = lax.axis_index("seq") * 2 + lax.axis_index("wsh")
        peer_of = group_peer
    else:
        me = lax.axis_index("ctx")
        peer_of = ctx_peer
    barrier = pltpu.get_barrier_semaphore()
    for step in range(1, size):
        pl.semaphore_signal(
            barrier, inc=1, device_id=peer_of(lax.rem(me + step, size)), device_id_type=MESH
        )
    pl.semaphore_wait(barrier, size - 1)
    copies = []
    for index, spread in enumerate(spreads):
        src, dst = sources[index], targets[index]
        for step in range(1, size):
            peer = lax.rem(me + step, size)
            copy = pltpu.make_async_remote_copy(
                src_ref=src.at[peer] if spread else src,
                dst_ref=dst.at[me],
                send_sem=send_sems.at[index, step - 1],
                recv_sem=recv_sems.at[index, step - 1],
                device_id=peer_of(peer),
                device_id_type=MESH,
            )
            copy.start()
            copies.append(copy)
        own = pltpu.make_async_copy(src.at[me] if spread else src, dst.at[me], own_sems.at[index])
        own.start()
        copies.append(own)
    for copy in copies:
        copy.wait()


def exchange(shards, size, group, spreads, number):
    count = len(shards)
    return pl.pallas_call(
        functools.partial(exchange_kernel, size, group, spreads),
        out_shape=[
            jax.ShapeDtypeStruct(x.shape if spread else (size,) + x.shape, x.dtype)
            for x, spread in zip(shards, spreads)
        ],
        in_specs=[pl.BlockSpec(memory_space=pl.ANY)] * count,
        out_specs=[pl.BlockSpec(memory_space=pl.ANY)] * count,
        scratch_shapes=[
            pltpu.SemaphoreType.DMA((count, size - 1)),
            pltpu.SemaphoreType.DMA((count, size - 1)),
            pltpu.SemaphoreType.DMA((count,)),
        ],
        compiler_params=pltpu.CompilerParams(collective_id=number, has_side_effects=True),
    )(*shards)


def square_places():
    seq, wsh = lax.axis_index("seq"), lax.axis_index("wsh")
    me = seq * 2 + wsh
    sibling = seq * 2 + 1 - wsh
    across = (1 - seq) * 2 + wsh
    corner = (1 - seq) * 2 + 1 - wsh
    return me, sibling, across, corner


def greet(peers, peer_of):
    barrier = pltpu.get_barrier_semaphore()
    for peer in peers:
        pl.semaphore_signal(barrier, inc=1, device_id=peer_of(peer), device_id_type=MESH)
    pl.semaphore_wait(barrier, len(peers))


def square_copy(source, target, sends, recvs, slot, peer):
    copy = pltpu.make_async_remote_copy(
        src_ref=source,
        dst_ref=target,
        send_sem=sends.at[slot],
        recv_sem=recvs.at[slot],
        device_id=group_peer(peer),
        device_id_type=MESH,
    )
    copy.start()
    return copy


def square_gather_kernel(src, dst, sends, recvs, own_sem):
    me, sibling, across, corner = square_places()
    greet([sibling, across], group_peer)
    far = square_copy(src, dst.at[me], sends, recvs, 0, across)
    near = square_copy(src, dst.at[me], sends, recvs, 1, sibling)
    own = pltpu.make_async_copy(src, dst.at[me], own_sem)
    own.start()
    far.wait()
    onward = square_copy(dst.at[across], dst.at[across], sends, recvs, 2, sibling)
    near.wait()
    own.wait()
    onward.wait()


def square_gather(shard, number):
    whole = pl.BlockSpec(memory_space=pltpu.VMEM)
    return pl.pallas_call(
        square_gather_kernel,
        out_shape=jax.ShapeDtypeStruct((4,) + shard.shape, shard.dtype),
        in_specs=[whole],
        out_specs=whole,
        scratch_shapes=[
            pltpu.SemaphoreType.DMA((3,)),
            pltpu.SemaphoreType.DMA((3,)),
            pltpu.SemaphoreType.DMA,
        ],
        compiler_params=pltpu.CompilerParams(
            collective_id=number, has_side_effects=True, vmem_limit_bytes=32 * 1024 * 1024
        ),
    )(shard)


def square_sum_kernel(src, out, held, sends, recvs):
    wide = jnp.float32
    rows = src.shape[1]
    block = 32 if rows % 32 == 0 else 16
    me, sibling, across, corner = square_places()
    greet([sibling, across], group_peer)
    first = square_copy(src.at[corner], held.at[0], sends, recvs, 0, sibling)
    near = square_copy(src.at[sibling], held.at[1], sends, recvs, 1, sibling)
    first.wait()

    def join(index, carry):
        at = pl.ds(pl.multiple_of(index * block, block), block)
        held[2, at, :] = (src[across, at, :].astype(wide) + held[0, at, :].astype(wide)).astype(
            held.dtype
        )
        return carry

    lax.fori_loop(0, rows // block, join, 0)
    far = square_copy(held.at[2], held.at[3], sends, recvs, 2, across)
    near.wait()
    far.wait()

    def finish(index, carry):
        at = pl.ds(pl.multiple_of(index * block, block), block)
        out[at, :] = (
            src[me, at, :].astype(wide) + held[1, at, :].astype(wide) + held[3, at, :].astype(wide)
        )
        return carry

    lax.fori_loop(0, rows // block, finish, 0)


def square_sum(terms, number):
    whole = pl.BlockSpec(memory_space=pltpu.VMEM)
    return pl.pallas_call(
        square_sum_kernel,
        out_shape=jax.ShapeDtypeStruct(terms.shape[1:], jnp.float32),
        in_specs=[whole],
        out_specs=whole,
        scratch_shapes=[
            pltpu.VMEM(terms.shape, terms.dtype),
            pltpu.SemaphoreType.DMA((3,)),
            pltpu.SemaphoreType.DMA((3,)),
        ],
        compiler_params=pltpu.CompilerParams(
            collective_id=number, has_side_effects=True, vmem_limit_bytes=32 * 1024 * 1024
        ),
    )(terms)


def rows_kernel(parts, pieces, grad, out):
    rows = out.shape[0]
    width = grad.shape[-1] // pieces
    for piece in range(pieces):
        for part in range(parts):
            start = (piece * parts + part) * width
            out[:, start : start + width] = grad[
                0, part * rows : (part + 1) * rows, piece * width : (piece + 1) * width
            ].astype(out.dtype)


def columns_kernel(grad, out):
    out[...] = grad[0].astype(out.dtype)


def reduce_kernel(turns, size, count, *refs):
    low, wide = jnp.bfloat16, jnp.float32
    refs = list(refs)
    gains = refs.pop(count)
    gain_out = refs.pop(2 * count)
    grads, outs = refs[:count], refs[count : 2 * count]
    from_y, from_z, total = (refs[(2 + i) * count : (3 + i) * count] for i in range(3))
    sends, recvs = refs[5 * count : 5 * count + 2]
    gain_in, gain_all, gain_sends, gain_recvs = refs[5 * count + 2 :]
    depth = size // 2
    parts = 4
    me = lax.axis_index("ctx")
    place, side = me // 2, lax.rem(me, 2)
    across = me + 1 - 2 * side
    group_me = lax.axis_index("seq") * 2 + lax.axis_index("wsh")
    z_peers = [lax.rem(place + step, depth) for step in range(1, depth)]
    x_peers = [lax.rem(group_me + step, parts) for step in range(1, parts)]

    ctx_peers = [lax.rem(me + step, size) for step in range(1, size)]
    barrier = pltpu.get_barrier_semaphore()
    for peer in ctx_peers:
        pl.semaphore_signal(barrier, inc=1, device_id=ctx_peer(peer), device_id_type=MESH)
    for peer in x_peers:
        pl.semaphore_signal(barrier, inc=1, device_id=group_peer(peer), device_id_type=MESH)
    pl.semaphore_wait(barrier, len(ctx_peers) + len(x_peers))

    def remote(chunk, slot, source, target, device):
        copy = pltpu.make_async_remote_copy(
            src_ref=source,
            dst_ref=target,
            send_sem=sends.at[chunk, slot],
            recv_sem=recvs.at[chunk, slot],
            device_id=device,
            device_id_type=MESH,
        )
        copy.start()
        return copy

    def by_rows(rows, step_body):
        block = 32 if rows % 32 == 0 else 16

        def body(index, carry):
            step_body(pl.ds(pl.multiple_of(index * block, block), block))
            return carry

        lax.fori_loop(0, rows // block, body, 0)

    z_slot = depth
    x_slot = z_slot + depth - 1
    zg_slot = x_slot + parts - 1
    yg_slot = zg_slot + depth - 1
    ys, zs, xs, zgs, ygs = ({} for _ in range(5))

    def start_y(c):
        ys[c] = [
            remote(c, z, grads[c].at[2 * z + 1 - side], from_y[c].at[z], ctx_peer(across))
            for z in range(depth)
        ]

    def start_z(c):
        rows = total[c].shape[0]
        for copy in ys[c]:
            copy.wait()

        def add(at):
            for z in range(depth):
                from_y[c][z, at, :] = (
                    grads[c][2 * z + side, at, :].astype(wide) + from_y[c][z, at, :].astype(wide)
                ).astype(low)

        by_rows(rows, add)
        zs[c] = [
            remote(
                c, z_slot + i, from_y[c].at[peer], from_z[c].at[place], ctx_peer(peer * 2 + side)
            )
            for i, peer in enumerate(z_peers)
        ]

    def start_x(c):
        rows = total[c].shape[0]
        for copy in zs[c]:
            copy.wait()

        def add(at):
            summed = from_y[c][place, at, :].astype(wide)
            for peer in z_peers:
                summed = summed + from_z[c][peer, at, :].astype(wide)
            if turns[c]:
                total[c][at, :] = summed.astype(low)
            else:
                outs[c][me, at, :] = summed.astype(low)

        by_rows(rows, add)
        if turns[c]:
            piece = rows // parts
            xs[c] = [
                remote(
                    c,
                    x_slot + i,
                    total[c].at[pl.ds(pl.multiple_of(peer * piece, piece), piece)],
                    outs[c].at[me, pl.ds(pl.multiple_of(group_me * piece, piece), piece)],
                    group_peer(peer),
                )
                for i, peer in enumerate(x_peers)
            ]
            mine = pl.ds(pl.multiple_of(group_me * piece, piece), piece)
            outs[c][me, mine, :] = total[c][mine, :]

    def start_zg(c):
        if turns[c]:
            for copy in xs[c]:
                copy.wait()
        zgs[c] = [
            remote(c, zg_slot + i, outs[c].at[me], outs[c].at[me], ctx_peer(peer * 2 + side))
            for i, peer in enumerate(z_peers)
        ]
        ygs[c] = [remote(c, yg_slot, outs[c].at[me], outs[c].at[me], ctx_peer(across))]

    def start_yg(c):
        for i, (copy, step) in enumerate(zip(zgs[c], range(1, depth))):
            copy.wait()
            came = lax.rem(place + depth - step, depth) * 2 + side
            ygs[c].append(
                remote(c, yg_slot + step, outs[c].at[came], outs[c].at[came], ctx_peer(across))
            )

    gain_copies = []
    for i, peer in enumerate(x_peers):
        gain_copies.append(
            pltpu.make_async_remote_copy(
                src_ref=gains.at[peer],
                dst_ref=gain_in.at[group_me],
                send_sem=gain_sends.at[i],
                recv_sem=gain_recvs.at[i],
                device_id=group_peer(peer),
                device_id_type=MESH,
            )
        )
        gain_copies[-1].start()
    for c in range(count):
        start_y(c)
    for copy in gain_copies:
        copy.wait()
    summed = gains[group_me]
    for peer in x_peers:
        summed = summed + gain_in[peer]
    gain_all[me] = summed
    gain_copies = []
    for i, peer in enumerate(ctx_peers):
        gain_copies.append(
            pltpu.make_async_remote_copy(
                src_ref=gain_all.at[me],
                dst_ref=gain_all.at[me],
                send_sem=gain_sends.at[parts - 1 + i],
                recv_sem=gain_recvs.at[parts - 1 + i],
                device_id=ctx_peer(peer),
                device_id_type=MESH,
            )
        )
        gain_copies[-1].start()
    for turn in range(count + 3):
        for stage, back in ((start_z, 0), (start_x, 1), (start_zg, 2), (start_yg, 3)):
            if 0 <= turn - back < count:
                stage(turn - back)
    for copy in gain_copies:
        copy.wait()
    summed = gain_all[0]
    for peer in range(1, size):
        summed = summed + gain_all[peer]
    gain_out[...] = summed
    for c in range(count):
        for copy in ygs[c]:
            copy.wait()


def reduce_over_ctx(grads, gains, turns, size, number):
    count = len(grads)
    depth = size // 2
    slots = depth + 2 * (depth - 1) + 3 + depth
    whole = pl.BlockSpec(memory_space=pltpu.VMEM)
    pairs = [pltpu.VMEM((depth,) + g.shape[1:], g.dtype) for g in grads]
    totals = [pltpu.VMEM(g.shape[1:], g.dtype) for g in grads]
    return pl.pallas_call(
        functools.partial(reduce_kernel, turns, size, count),
        out_shape=[jax.ShapeDtypeStruct(g.shape, g.dtype) for g in grads]
        + [jax.ShapeDtypeStruct(gains.shape[1:], gains.dtype)],
        in_specs=[whole] * (count + 1),
        out_specs=[whole] * (count + 1),
        scratch_shapes=pairs
        + pairs
        + totals
        + [
            pltpu.SemaphoreType.DMA((count, slots)),
            pltpu.SemaphoreType.DMA((count, slots)),
            pltpu.VMEM(gains.shape, gains.dtype),
            pltpu.VMEM((size,) + gains.shape[1:], gains.dtype),
            pltpu.SemaphoreType.DMA((size + 2,)),
            pltpu.SemaphoreType.DMA((size + 2,)),
        ],
        compiler_params=pltpu.CompilerParams(
            collective_id=number, has_side_effects=True, vmem_limit_bytes=48 * 1024 * 1024
        ),
    )(*grads, gains)


def permute_group(chunk_for, parts):
    me = lax.axis_index(GROUP)
    came = [chunk_for(me)]
    for step in range(1, parts):
        pairs = [(i, i ^ step) for i in range(parts)]
        came.append(lax.ppermute(chunk_for(me ^ step), GROUP, pairs))
    return came


def layer_norm_parts(values):
    middle = jnp.mean(values, -1, keepdims=True)
    centred = values - middle
    factor = lax.rsqrt(jnp.mean(centred * centred, -1, keepdims=True) + layer_eps)
    return centred * factor, factor


def norm_back(grad, gain, normed, factor):
    scaled = grad * gain
    return factor * (
        scaled
        - jnp.mean(scaled, -1, keepdims=True)
        - normed * jnp.mean(scaled * normed, -1, keepdims=True)
    )


def dot(equation, left, right):
    return jnp.einsum(equation, left, right, preferred_element_type=jnp.float32)


def parallel(parts, ctx_size, tokens, positions, w_qkv, w_out, w_in, w_down, gain_attn, gain_mlp,
             cotangent):
    low = jnp.bfloat16
    wide = jnp.float32
    row_count = tokens.shape[1]
    length = row_count * ctx_size
    part_heads = HEADS // parts
    part_ff = FF // parts
    part_d = D // parts
    pairs = parts * part_heads // ctx_size
    seq_split = part_heads // pairs
    half = HEAD // 2
    scaling = HEAD ** (-0.5)
    ctx_index = lax.axis_index("ctx")

    gather = square_gather

    def swap_ctx(shard, number):
        return exchange([shard], ctx_size, False, (True,), number)[0]

    inputs = tokens[0].astype(wide)
    cot = cotangent[0]
    small = jnp.concatenate(
        [positions[0].astype(wide), gain_attn.astype(wide), gain_mlp.astype(wide)]
    )
    qkv_split = w_qkv.reshape(part_d, 3, parts, part_d).transpose(2, 0, 1, 3)
    small, all_tokens, qkv_cols = exchange(
        [small.reshape(-1, 128), tokens[0], qkv_split.reshape(parts, part_d, 3 * part_d)],
        parts,
        True,
        (False, False, True),
        1,
    )
    small = small.reshape(parts, -1)
    qkv_cols = qkv_cols.reshape(D, 3 * part_d)
    w_in, cot_sent, small = lax.optimization_barrier((w_in, cot, small))
    gain_one = small[:, row_count : row_count + part_d].reshape(D)
    gain_two = small[:, row_count + part_d :].reshape(D)
    all_positions = (
        exchange([small[:, :row_count].astype(jnp.int32)], ctx_size, False, (False,), 26)[0]
        .transpose(1, 0, 2)
        .reshape(parts, length)
    )
    starts = jnp.arange(length, dtype=jnp.int32)[None, :] - all_positions
    group_positions = lax.dynamic_slice_in_dim(all_positions, ctx_index * row_count, row_count, 1)
    my_seq = ctx_index // seq_split
    seq_positions = lax.dynamic_index_in_dim(all_positions, my_seq, 0, False)
    seq_starts = lax.dynamic_index_in_dim(starts, my_seq, 0, False)

    relative = jnp.arange(parts) ^ lax.axis_index(GROUP)

    def in_chunk(peer):
        return jnp.concatenate(
            [
                lax.dynamic_slice_in_dim(w_in, half_at + peer * part_ff, part_ff, 1)
                for half_at in (0, FF)
            ],
            1,
        )

    in_cols = jnp.concatenate(permute_group(in_chunk, parts))
    all_cot = jnp.stack(permute_group(lambda peer: cot_sent, parts))[relative]
    norm_one, factor_one = layer_norm_parts(inputs)
    normed_attn = (layer_norm_parts(all_tokens.astype(wide))[0] * gain_one).astype(low)
    projected = dot("stc,cf->stf", normed_attn, qkv_cols)
    cosine, sine = rotary_tables(group_positions)
    turned = [
        rotate(
            projected[..., i * part_d : (i + 1) * part_d].reshape(
                parts, row_count, part_heads, HEAD
            ),
            cosine,
            sine,
        )
        for i in range(2)
    ]
    turned.append(projected[..., 2 * part_d :].reshape(parts, row_count, part_heads, HEAD))
    heads_out = jnp.stack([t.astype(low) for t in turned])
    heads_out = (
        heads_out.reshape(3, parts, row_count, seq_split, pairs * HEAD)
        .transpose(1, 3, 2, 0, 4)
        .reshape(ctx_size, row_count, 3 * pairs * HEAD)
    )
    heads_in = swap_ctx(heads_out, 3).reshape(length, 3, pairs, HEAD).transpose(1, 2, 0, 3)
    queries, keys, values = heads_in
    same = (seq_starts[:, None] == seq_starts[None, :])[None]
    scores = jnp.where(same, dot("hqd,hkd->hqk", queries, keys) * scaling, far_below)
    best = jnp.max(scores, -1, keepdims=True)
    raised = jnp.where(same, jnp.exp(scores - best), 0.0)
    totals = jnp.sum(raised, -1, keepdims=True)
    log_total = best + jnp.log(totals)
    attended = dot("hqk,hkd->hqd", raised.astype(low), values) / totals

    def to_tokens(shard, width):
        return (
            shard.transpose(1, 0, 2).reshape(ctx_size, row_count, pairs * width)
        )

    def from_ctx(shard):
        return (
            shard.reshape(parts, seq_split, row_count, -1)
            .transpose(0, 2, 1, 3)
            .reshape(parts, row_count, -1)
        )

    attended_low = from_ctx(swap_ctx(to_tokens(attended.astype(low), HEAD), 4))
    mixed = inputs + square_sum(dot("stc,cf->stf", attended_low, w_out).astype(low), 5)
    norm_two, factor_two = layer_norm_parts(mixed)
    normed_mlp = gather((norm_two * gain_two).astype(low), 6)
    turned_mlp = normed_mlp.reshape(parts, row_count, parts, part_d)[:, :, relative]
    hidden = dot("stc,cf->stf", turned_mlp.reshape(normed_mlp.shape), in_cols)
    inner, gate = hidden[..., :part_ff], hidden[..., part_ff:]
    product, pull = jax.vjp(geglu, inner, gate)
    product = product.astype(low)
    grad_product = dot("stn,fn->stf", all_cot, w_down)
    grad_inner, grad_gate = pull(grad_product)
    grad_hidden = jnp.concatenate([grad_inner, grad_gate], -1).astype(low)
    normed_back = dot("stf,cf->stc", grad_hidden, in_cols).astype(low)
    normed_back = normed_back.reshape(parts, row_count, parts, part_d)[:, :, relative]
    grad_normed_mlp = square_sum(normed_back.reshape(normed_mlp.shape), 9)
    grad_gain_mlp = jnp.sum(grad_normed_mlp * norm_two, 0)
    grad_mixed = cot.astype(wide) + norm_back(grad_normed_mlp, gain_two, norm_two, factor_two)
    grad_branch = gather(grad_mixed.astype(low), 10)
    grad_attended = dot("stf,cf->stc", grad_branch, w_out).astype(low)
    grad_out = (
        grad_attended.reshape(parts, row_count, seq_split, pairs * HEAD)
        .transpose(0, 2, 1, 3)
        .reshape(ctx_size, row_count, pairs * HEAD)
    )
    grad_heads = swap_ctx(grad_out, 11).reshape(length, pairs, HEAD).transpose(1, 0, 2)

    output_parts = dot("stf,fn->stn", product, w_down).astype(low)
    output_parts, grad_branch = lax.optimization_barrier((output_parts, grad_branch))
    output_parts = permute_group(
        lambda peer: lax.dynamic_index_in_dim(output_parts, peer, 0, False), parts
    )
    output = (mixed + sum(part.astype(wide) for part in output_parts)).astype(low)

    def rows_of(grad, width):
        return (
            grad.reshape(parts, ctx_size, part_d // ctx_size, width)
            .transpose(1, 0, 2, 3)
            .reshape(ctx_size, -1, width)
            .astype(low)
        )

    def columns_of(grad):
        rows = grad.shape[0]
        return grad.reshape(rows, ctx_size, D // ctx_size).transpose(1, 0, 2).astype(low)

    def back_to_rows(grad, pieces):
        rows = part_d // ctx_size
        width = parts * grad.shape[-1]
        return pl.pallas_call(
            functools.partial(rows_kernel, parts, pieces),
            grid=(ctx_size,),
            out_shape=jax.ShapeDtypeStruct((part_d, width), wide),
            in_specs=[pl.BlockSpec((1,) + grad.shape[1:], lambda i: (i, 0, 0))],
            out_specs=pl.BlockSpec((rows, width), lambda i: (i, 0)),
        )(grad)

    def back_to_columns(grad):
        rows, width = grad.shape[1:]
        return pl.pallas_call(
            columns_kernel,
            grid=(ctx_size,),
            out_shape=jax.ShapeDtypeStruct((rows, D), wide),
            in_specs=[pl.BlockSpec((1, rows, width), lambda i: (i, 0, 0))],
            out_specs=pl.BlockSpec((rows, width), lambda i: (0, i)),
        )(grad)

    down_grad = columns_of(dot("stf,stn->fn", product, all_cot))
    in_grad = rows_of(dot("stc,stf->cf", normed_mlp, grad_hidden), 2 * part_ff)

    row_dot = jnp.sum(grad_heads.astype(wide) * attended, -1, keepdims=True)
    weights_f = jnp.where(same, jnp.exp(scores - log_total), 0.0)
    grad_weights = dot("hqd,hkd->hqk", grad_heads, values)
    grad_scores = (weights_f * (grad_weights - row_dot)).astype(low)
    grad_queries = dot("hqk,hkd->hqd", grad_scores, keys) * scaling
    grad_keys = dot("hqk,hqd->hkd", grad_scores, queries) * scaling
    grad_values = dot("hqk,hqd->hkd", weights_f.astype(low), grad_heads)
    seq_cos, seq_sin = rotary_tables(seq_positions)
    seq_cos, seq_sin = seq_cos[:, 0][None], seq_sin[:, 0][None]
    grads = jnp.stack(
        [
            rotate_back(grad_queries, seq_cos, seq_sin),
            rotate_back(grad_keys, seq_cos, seq_sin),
            grad_values,
        ]
    ).astype(low)
    grads = grads.transpose(2, 0, 1, 3).reshape(ctx_size, row_count, 3 * pairs * HEAD)
    grads = swap_ctx(grads, 15)
    grad_projected = (
        grads.reshape(parts, seq_split, row_count, 3, pairs * HEAD)
        .transpose(0, 2, 3, 1, 4)
        .reshape(parts, row_count, 3 * part_d)
    )
    grad_normed_attn = square_sum(dot("stf,cf->stc", grad_projected, qkv_cols).astype(low), 16)
    grad_gain_attn = jnp.sum(grad_normed_attn * norm_one, 0)
    grad_tokens = (
        grad_mixed + norm_back(grad_normed_attn, gain_one, norm_one, factor_one)
    ).astype(low)

    out_grad = columns_of(dot("stc,stf->cf", attended_low, grad_branch))
    qkv_grad = rows_of(dot("stc,stf->cf", normed_attn, grad_projected), 3 * part_d)
    gain_sums = jnp.stack([grad_gain_attn, grad_gain_mlp]).reshape(2, parts, part_d)
    out_grad, down_grad, qkv_grad, in_grad, gain_sums = reduce_over_ctx(
        [out_grad, down_grad, qkv_grad, in_grad],
        gain_sums.transpose(1, 0, 2),
        (False, False, True, True),
        ctx_size,
        13,
    )
    return (
        output[None],
        grad_tokens[None],
        back_to_rows(qkv_grad, 3),
        back_to_columns(out_grad),
        back_to_rows(in_grad, 2),
        back_to_columns(down_grad),
        gain_sums[0],
        gain_sums[1],
    )


def solution(mesh):
    placed = (
        P(("seq", "wsh"), "ctx", None),
        P(("seq", "wsh"), "ctx"),
        P(("seq", "wsh"), None),
        P(("seq", "wsh"), None),
        P(("seq", "wsh"), None),
        P(("seq", "wsh"), None),
        P(("seq", "wsh")),
        P(("seq", "wsh")),
        P(("seq", "wsh"), "ctx", None),
    )
    parts = mesh.shape["seq"] * mesh.shape["wsh"]
    ctx_size = mesh.shape["ctx"]
    whole_pairs = HEADS % ctx_size == 0 and ctx_size % 2 == 0 and parts == 4
    body = functools.partial(parallel, parts, ctx_size) if whole_pairs else local
    return jax.shard_map(
        body,
        mesh=mesh,
        in_specs=placed,
        out_specs=(
            P(("seq", "wsh"), "ctx", None),
            P(("seq", "wsh"), "ctx", None),
            P(("seq", "wsh"), None),
            P(("seq", "wsh"), None),
            P(("seq", "wsh"), None),
            P(("seq", "wsh"), None),
            P(("seq", "wsh")),
            P(("seq", "wsh")),
        ),
        check_vma=False,
    )
```

```python
import functools
import math

import jax
import jax.numpy as jnp
from jax import lax
from jax.experimental import pallas as pl
from jax.experimental.pallas import tpu as pltpu
from jax.sharding import PartitionSpec as P

D = 1024
HEADS = 16
HEAD = 64
FF = 2624


layer_eps = 1e-05
rope_base = 160000.0
far_below = -1e30


def from_behind(shard, axis, by):
    size = lax.axis_size(axis)
    return lax.ppermute(shard, axis, [(i, (i + by) % size) for i in range(size)])


def normalize(values, gain_vector):
    middle = jnp.mean(values, -1, keepdims=True)
    centred = values - middle
    spread = jnp.mean(centred * centred, -1, keepdims=True)
    return centred * lax.rsqrt(spread + layer_eps) * gain_vector


def rotary_tables(positions):
    half_size = HEAD // 2
    frequency = jnp.exp(
        jnp.arange(half_size, dtype=jnp.float32) * (-2.0 * math.log(rope_base) / HEAD)
    )
    angles = positions.astype(jnp.float32)[..., None] * frequency
    cosine = jnp.cos(angles)
    sine_table = jnp.sin(angles)
    return (
        jnp.concatenate([cosine, cosine], -1)[..., None, :],
        jnp.concatenate([sine_table, sine_table], -1)[..., None, :],
    )


def rotate(values, cosine, sine_table):
    half_size = values.shape[-1] // 2
    turned = jnp.concatenate([-values[..., half_size:], values[..., :half_size]], -1)
    return values * cosine + turned * sine_table


def rotate_back(grads, cosine, sine_table):
    half_size = grads.shape[-1] // 2
    shifted = grads * sine_table
    return grads * cosine + jnp.concatenate(
        [shifted[..., half_size:], -shifted[..., :half_size]], -1
    )


def geglu(inner_part, gate_part):
    return jax.nn.gelu(inner_part, approximate=False) * gate_part


def same_document(query_starts, key_starts):
    return (query_starts[:, :, None] == key_starts[:, None, :])[:, :, None, :]


def fold_keys(queries, query_starts, scaling, running, piece):
    key_piece, value_piece, start_piece = piece
    seq_count = key_piece.shape[0]
    row_total = key_piece.shape[1]
    block_size = math.gcd(row_total, 512)

    def one_block(block_index, carried):
        best_score, totals, weighted = carried
        key_block = lax.dynamic_slice_in_dim(
            key_piece, block_index * block_size, block_size, 1
        ).reshape(seq_count, block_size, HEADS, HEAD)
        value_block = lax.dynamic_slice_in_dim(
            value_piece, block_index * block_size, block_size, 1
        ).reshape(seq_count, block_size, HEADS, HEAD)
        start_block = lax.dynamic_slice_in_dim(start_piece, block_index * block_size, block_size, 1)
        same_doc = same_document(query_starts, start_block)
        scores = (
            jnp.einsum("sqhd,skhd->sqhk", queries, key_block, preferred_element_type=jnp.float32)
            * scaling
        )
        scores = jnp.where(same_doc, scores, far_below)
        new_best = jnp.maximum(best_score, jnp.max(scores, -1))
        fading = jnp.exp(best_score - new_best)
        raised = jnp.where(same_doc, jnp.exp(scores - new_best[..., None]), 0.0)
        totals = totals * fading + jnp.sum(raised, -1)
        weighted = weighted * fading[..., None] + jnp.einsum(
            "sqhk,skhd->sqhd",
            raised.astype(jnp.bfloat16),
            value_block,
            preferred_element_type=jnp.float32,
        )
        return (new_best, totals, weighted)

    return lax.fori_loop(0, row_total // block_size, one_block, running)


def block_grads(
    queries,
    query_starts,
    key_block,
    value_block,
    key_starts,
    grad_split,
    log_total,
    row_dot,
    scaling,
):
    same_doc = same_document(query_starts, key_starts)
    scores = (
        jnp.einsum("sqhd,skhd->sqhk", queries, key_block, preferred_element_type=jnp.float32)
        * scaling
    )
    weights_f = jnp.where(same_doc, jnp.exp(scores - log_total[..., None]), 0.0)
    grad_weights = jnp.einsum(
        "sqhd,skhd->sqhk", grad_split, value_block, preferred_element_type=jnp.float32
    )
    grad_scores = (weights_f * (grad_weights - row_dot[..., None])).astype(jnp.bfloat16)
    grad_query = (
        jnp.einsum("sqhk,skhd->sqhd", grad_scores, key_block, preferred_element_type=jnp.float32)
        * scaling
    )
    grad_key = (
        jnp.einsum("sqhk,sqhd->skhd", grad_scores, queries, preferred_element_type=jnp.float32)
        * scaling
    )
    grad_value = jnp.einsum(
        "sqhk,sqhd->skhd",
        weights_f.astype(jnp.bfloat16),
        grad_split,
        preferred_element_type=jnp.float32,
    )
    return (grad_query, grad_key, grad_value)


def local(tokens, positions, w_qkv, w_out, w_in, w_down, gain_attn, gain_mlp, cotangent):
    seq_count = tokens.shape[0]
    row_count = tokens.shape[1]
    scaling = HEAD ** (-0.5)
    split_shape = (seq_count, row_count, HEADS, HEAD)
    flat_shape = (seq_count, row_count, D)
    (
        forward_query_weight,
        forward_out_weight,
        forward_in_weight,
        forward_down_weight,
        full_ga,
        full_gm,
    ) = (
        lax.all_gather(w_qkv, ("seq", "wsh"), axis=0, tiled=True),
        lax.all_gather(w_out, ("seq", "wsh"), axis=0, tiled=True),
        lax.all_gather(w_in, ("seq", "wsh"), axis=0, tiled=True),
        lax.all_gather(w_down, ("seq", "wsh"), axis=0, tiled=True),
        lax.all_gather(gain_attn, ("seq", "wsh"), axis=0, tiled=True),
        lax.all_gather(gain_mlp, ("seq", "wsh"), axis=0, tiled=True),
    )
    cosine, sine_table = rotary_tables(positions)
    token_index = lax.axis_index("ctx") * row_count + jnp.arange(row_count, dtype=jnp.int32)
    own_starts = token_index[None, :] - positions
    input_widened = tokens.astype(jnp.float32)
    gain_one = full_ga.astype(jnp.float32)
    gain_two = full_gm.astype(jnp.float32)
    attention_normed = normalize(input_widened, gain_one).astype(jnp.bfloat16)
    projected_output = jnp.einsum(
        "kch,hf->kcf", attention_normed, forward_query_weight, preferred_element_type=jnp.float32
    )
    queries = rotate(projected_output[..., :D].reshape(split_shape), cosine, sine_table).astype(
        jnp.bfloat16
    )
    key_rows = (
        rotate(projected_output[..., D : 2 * D].reshape(split_shape), cosine, sine_table)
        .astype(jnp.bfloat16)
        .reshape(flat_shape)
    )
    value_rows = projected_output[..., 2 * D :].astype(jnp.bfloat16)
    start_state = (
        jnp.full((seq_count, row_count, HEADS), far_below, jnp.float32),
        jnp.zeros((seq_count, row_count, HEADS), jnp.float32),
        jnp.zeros(split_shape, jnp.float32),
    )
    best_score, totals, weighted = fold_keys(
        queries,
        own_starts,
        scaling,
        start_state,
        (
            lax.all_gather(key_rows, "ctx", axis=1, tiled=True),
            lax.all_gather(value_rows, "ctx", axis=1, tiled=True),
            lax.all_gather(own_starts, "ctx", axis=1, tiled=True),
        ),
    )
    attended = weighted / totals[..., None]
    log_total = best_score + jnp.log(totals)
    attended_reduced = attended.reshape(flat_shape).astype(jnp.bfloat16)
    mixed_token_rows = input_widened + jnp.einsum(
        "kch,hf->kcf", attended_reduced, forward_out_weight, preferred_element_type=jnp.float32
    )
    feedforward_normed = normalize(mixed_token_rows, gain_two).astype(jnp.bfloat16)
    hidden_state = jnp.einsum(
        "rnk,kx->rnx", feedforward_normed, forward_in_weight, preferred_element_type=jnp.float32
    )
    inner_part = hidden_state[..., :FF]
    gate_part = hidden_state[..., FF:]
    gated_product = geglu(inner_part, gate_part).astype(jnp.bfloat16)
    output = (
        mixed_token_rows
        + jnp.einsum(
            "ogw,wn->ogn", gated_product, forward_down_weight, preferred_element_type=jnp.float32
        )
    ).astype(jnp.bfloat16)
    backward_query_weight, backward_out_weight, backward_in_weight, backward_down_weight = (
        forward_query_weight,
        forward_out_weight,
        forward_in_weight,
        forward_down_weight,
    )
    down_weight_gradient = jnp.einsum(
        "xvt,xvw->tw", gated_product, cotangent, preferred_element_type=jnp.float32
    )
    grad_product = jnp.einsum(
        "xzi,mi->xzm", cotangent, backward_down_weight, preferred_element_type=jnp.float32
    )
    geglu_pull = jax.vjp(geglu, inner_part, gate_part)[1]
    grad_inner, grad_gate = geglu_pull(grad_product)
    hidden_gradient = jnp.concatenate([grad_inner, grad_gate], -1).astype(jnp.bfloat16)
    grad_w_in = jnp.einsum(
        "hrq,hrw->qw", feedforward_normed, hidden_gradient, preferred_element_type=jnp.float32
    )
    grad_normed_mlp = jnp.einsum(
        "xcu,au->xca", hidden_gradient, backward_in_weight, preferred_element_type=jnp.float32
    )
    mlp_pull = jax.vjp(normalize, mixed_token_rows, gain_two)[1]
    grad_mixed_norm, grad_gain_mlp = mlp_pull(grad_normed_mlp)
    grad_mixed = cotangent.astype(jnp.float32) + grad_mixed_norm
    branch_gradient = grad_mixed.astype(jnp.bfloat16)
    grad_w_out = jnp.einsum(
        "pgj,pgv->jv", attended_reduced, branch_gradient, preferred_element_type=jnp.float32
    )
    grad_attended = jnp.einsum(
        "arq,xq->arx", branch_gradient, backward_out_weight, preferred_element_type=jnp.float32
    ).astype(jnp.bfloat16)
    grad_split = grad_attended.reshape(split_shape)
    row_dot = jnp.sum(grad_split.astype(jnp.float32) * attended, -1)
    cycle_turns = lax.axis_size("ctx") - 1
    zeros_flat = jnp.zeros(flat_shape, jnp.float32)

    def key_turn(turn_index, carried):
        moving_keys, moving_values, moving_starts, grad_keys, grad_values, grad_queries = carried
        grad_query, grad_key, grad_value = block_grads(
            queries,
            own_starts,
            moving_keys.reshape(split_shape),
            moving_values.reshape(split_shape),
            moving_starts,
            grad_split,
            log_total,
            row_dot,
            scaling,
        )
        moving_keys, moving_values, moving_starts = from_behind(
            (moving_keys, moving_values, moving_starts), "ctx", 1
        )
        grad_keys, grad_values = (
            from_behind(
                (grad_keys + grad_key.reshape(flat_shape)).astype(jnp.bfloat16), "ctx", 1
            ).astype(jnp.float32),
            from_behind(
                (grad_values + grad_value.reshape(flat_shape)).astype(jnp.bfloat16), "ctx", 1
            ).astype(jnp.float32),
        )
        return (
            moving_keys,
            moving_values,
            moving_starts,
            grad_keys,
            grad_values,
            grad_queries + grad_query,
        )

    moving_keys, moving_values, moving_starts, grad_keys, grad_values, grad_queries = lax.fori_loop(
        0,
        cycle_turns,
        key_turn,
        (
            key_rows,
            value_rows,
            own_starts,
            zeros_flat,
            zeros_flat,
            jnp.zeros(split_shape, jnp.float32),
        ),
    )
    grad_query, grad_key, grad_value = block_grads(
        queries,
        own_starts,
        moving_keys.reshape(split_shape),
        moving_values.reshape(split_shape),
        moving_starts,
        grad_split,
        log_total,
        row_dot,
        scaling,
    )
    grad_queries = grad_queries + grad_query
    grad_keys, grad_values = (
        from_behind(
            (grad_keys + grad_key.reshape(flat_shape)).astype(jnp.bfloat16), "ctx", 1
        ).astype(jnp.float32),
        from_behind(
            (grad_values + grad_value.reshape(flat_shape)).astype(jnp.bfloat16), "ctx", 1
        ).astype(jnp.float32),
    )
    projected_gradient = jnp.concatenate(
        [
            rotate_back(grad_queries, cosine, sine_table).reshape(flat_shape),
            rotate_back(grad_keys.reshape(split_shape), cosine, sine_table).reshape(flat_shape),
            grad_values,
        ],
        -1,
    ).astype(jnp.bfloat16)
    grad_w_qkv = jnp.einsum(
        "pgj,pgv->jv", attention_normed, projected_gradient, preferred_element_type=jnp.float32
    )
    grad_normed_attn = jnp.einsum(
        "arq,xq->arx", projected_gradient, backward_query_weight, preferred_element_type=jnp.float32
    )
    attn_pull = jax.vjp(normalize, input_widened, gain_one)[1]
    grad_inputs_norm, grad_gain_attn = attn_pull(grad_normed_attn)
    grad_tokens = (grad_mixed + grad_inputs_norm).astype(jnp.bfloat16)
    shares = (
        lax.psum_scatter(
            grad_w_qkv.astype(jnp.bfloat16), ("seq", "wsh"), scatter_dimension=0, tiled=True
        ).astype(jnp.float32),
        lax.psum_scatter(
            grad_w_out.astype(jnp.bfloat16), ("seq", "wsh"), scatter_dimension=0, tiled=True
        ).astype(jnp.float32),
        lax.psum_scatter(
            grad_w_in.astype(jnp.bfloat16), ("seq", "wsh"), scatter_dimension=0, tiled=True
        ).astype(jnp.float32),
        lax.psum_scatter(
            down_weight_gradient.astype(jnp.bfloat16),
            ("seq", "wsh"),
            scatter_dimension=0,
            tiled=True,
        ).astype(jnp.float32),
        lax.psum_scatter(
            grad_gain_attn.astype(jnp.bfloat16), ("seq", "wsh"), scatter_dimension=0, tiled=True
        ).astype(jnp.float32),
        lax.psum_scatter(
            grad_gain_mlp.astype(jnp.bfloat16), ("seq", "wsh"), scatter_dimension=0, tiled=True
        ).astype(jnp.float32),
    )
    summed = lax.psum((shares[0], shares[1], shares[2], shares[3], shares[4], shares[5]), "ctx")
    return (output, grad_tokens, summed[0], summed[1], summed[2], summed[3], summed[4], summed[5])


GROUP = ("seq", "wsh")
MESH = pl.DeviceIdType.MESH


def group_peer(index):
    return {"seq": index // 2, "wsh": lax.rem(index, 2)}


def ctx_peer(index):
    return {"ctx": index}


def exchange_kernel(size, group, spreads, *refs):
    count = len(spreads)
    sources, targets = refs[:count], refs[count : 2 * count]
    send_sems, recv_sems, own_sems = refs[2 * count :]
    if group:
        me = lax.axis_index("seq") * 2 + lax.axis_index("wsh")
        peer_of = group_peer
    else:
        me = lax.axis_index("ctx")
        peer_of = ctx_peer
    barrier = pltpu.get_barrier_semaphore()
    for step in range(1, size):
        pl.semaphore_signal(
            barrier, inc=1, device_id=peer_of(lax.rem(me + step, size)), device_id_type=MESH
        )
    pl.semaphore_wait(barrier, size - 1)
    copies = []
    for index, spread in enumerate(spreads):
        src, dst = sources[index], targets[index]
        for step in range(1, size):
            peer = lax.rem(me + step, size)
            copy = pltpu.make_async_remote_copy(
                src_ref=src.at[peer] if spread else src,
                dst_ref=dst.at[me],
                send_sem=send_sems.at[index, step - 1],
                recv_sem=recv_sems.at[index, step - 1],
                device_id=peer_of(peer),
                device_id_type=MESH,
            )
            copy.start()
            copies.append(copy)
        own = pltpu.make_async_copy(src.at[me] if spread else src, dst.at[me], own_sems.at[index])
        own.start()
        copies.append(own)
    for copy in copies:
        copy.wait()


def exchange(shards, size, group, spreads, number):
    count = len(shards)
    return pl.pallas_call(
        functools.partial(exchange_kernel, size, group, spreads),
        out_shape=[
            jax.ShapeDtypeStruct(x.shape if spread else (size,) + x.shape, x.dtype)
            for x, spread in zip(shards, spreads)
        ],
        in_specs=[pl.BlockSpec(memory_space=pl.ANY)] * count,
        out_specs=[pl.BlockSpec(memory_space=pl.ANY)] * count,
        scratch_shapes=[
            pltpu.SemaphoreType.DMA((count, size - 1)),
            pltpu.SemaphoreType.DMA((count, size - 1)),
            pltpu.SemaphoreType.DMA((count,)),
        ],
        compiler_params=pltpu.CompilerParams(collective_id=number, has_side_effects=True),
    )(*shards)


def square_places():
    seq, wsh = lax.axis_index("seq"), lax.axis_index("wsh")
    me = seq * 2 + wsh
    sibling = seq * 2 + 1 - wsh
    across = (1 - seq) * 2 + wsh
    corner = (1 - seq) * 2 + 1 - wsh
    return me, sibling, across, corner


def greet(peers, peer_of):
    barrier = pltpu.get_barrier_semaphore()
    for peer in peers:
        pl.semaphore_signal(barrier, inc=1, device_id=peer_of(peer), device_id_type=MESH)
    pl.semaphore_wait(barrier, len(peers))


def square_copy(source, target, sends, recvs, slot, peer):
    copy = pltpu.make_async_remote_copy(
        src_ref=source,
        dst_ref=target,
        send_sem=sends.at[slot],
        recv_sem=recvs.at[slot],
        device_id=group_peer(peer),
        device_id_type=MESH,
    )
    copy.start()
    return copy


def square_gather_kernel(src, dst, sends, recvs, own_sem):
    me, sibling, across, corner = square_places()
    greet([sibling, across], group_peer)
    far = square_copy(src, dst.at[me], sends, recvs, 0, across)
    near = square_copy(src, dst.at[me], sends, recvs, 1, sibling)
    own = pltpu.make_async_copy(src, dst.at[me], own_sem)
    own.start()
    far.wait()
    onward = square_copy(dst.at[across], dst.at[across], sends, recvs, 2, sibling)
    near.wait()
    own.wait()
    onward.wait()


def square_gather(shard, number):
    whole = pl.BlockSpec(memory_space=pltpu.VMEM)
    return pl.pallas_call(
        square_gather_kernel,
        out_shape=jax.ShapeDtypeStruct((4,) + shard.shape, shard.dtype),
        in_specs=[whole],
        out_specs=whole,
        scratch_shapes=[
            pltpu.SemaphoreType.DMA((3,)),
            pltpu.SemaphoreType.DMA((3,)),
            pltpu.SemaphoreType.DMA,
        ],
        compiler_params=pltpu.CompilerParams(
            collective_id=number, has_side_effects=True, vmem_limit_bytes=32 * 1024 * 1024
        ),
    )(shard)


def square_sum_kernel(src, out, held, sends, recvs):
    wide = jnp.float32
    rows = src.shape[1]
    block = 32 if rows % 32 == 0 else 16
    me, sibling, across, corner = square_places()
    greet([sibling, across], group_peer)
    first = square_copy(src.at[corner], held.at[0], sends, recvs, 0, sibling)
    near = square_copy(src.at[sibling], held.at[1], sends, recvs, 1, sibling)
    first.wait()

    def join(index, carry):
        at = pl.ds(pl.multiple_of(index * block, block), block)
        held[2, at, :] = (src[across, at, :].astype(wide) + held[0, at, :].astype(wide)).astype(
            held.dtype
        )
        return carry

    lax.fori_loop(0, rows // block, join, 0)
    far = square_copy(held.at[2], held.at[3], sends, recvs, 2, across)
    near.wait()
    far.wait()

    def finish(index, carry):
        at = pl.ds(pl.multiple_of(index * block, block), block)
        out[at, :] = (
            src[me, at, :].astype(wide) + held[1, at, :].astype(wide) + held[3, at, :].astype(wide)
        )
        return carry

    lax.fori_loop(0, rows // block, finish, 0)


def square_sum(terms, number):
    whole = pl.BlockSpec(memory_space=pltpu.VMEM)
    return pl.pallas_call(
        square_sum_kernel,
        out_shape=jax.ShapeDtypeStruct(terms.shape[1:], jnp.float32),
        in_specs=[whole],
        out_specs=whole,
        scratch_shapes=[
            pltpu.VMEM(terms.shape, terms.dtype),
            pltpu.SemaphoreType.DMA((3,)),
            pltpu.SemaphoreType.DMA((3,)),
        ],
        compiler_params=pltpu.CompilerParams(
            collective_id=number, has_side_effects=True, vmem_limit_bytes=32 * 1024 * 1024
        ),
    )(terms)


def place_kernel(parts, pieces, *refs):
    count = len(pieces)
    for count_of, grad, out in zip(pieces, refs[:count], refs[count:]):
        if not count_of:
            out[...] = grad[0].astype(out.dtype)
            continue
        rows = out.shape[0]
        width = grad.shape[-1] // count_of
        for piece in range(count_of):
            for part in range(parts):
                start = (piece * parts + part) * width
                out[:, start : start + width] = grad[
                    0, part * rows : (part + 1) * rows, piece * width : (piece + 1) * width
                ].astype(out.dtype)


def reduce_kernel(turns, ready, size, count, *refs):
    low, wide = jnp.bfloat16, jnp.float32
    refs = list(refs)
    gains = refs.pop(count)
    gain_out = refs.pop(2 * count)
    grads, outs = refs[:count], refs[count : 2 * count]
    from_y, from_z, total = (refs[(2 + i) * count : (3 + i) * count] for i in range(3))
    sends, recvs = refs[5 * count : 5 * count + 2]
    gain_in, gain_all, gain_sends, gain_recvs = refs[5 * count + 2 :]
    depth = size // 2
    parts = 4
    me = lax.axis_index("ctx")
    place, side = me // 2, lax.rem(me, 2)
    across = me + 1 - 2 * side
    group_me = lax.axis_index("seq") * 2 + lax.axis_index("wsh")
    z_peers = [lax.rem(place + step, depth) for step in range(1, depth)]
    x_peers = [lax.rem(group_me + step, parts) for step in range(1, parts)]

    ctx_peers = [lax.rem(me + step, size) for step in range(1, size)]
    barrier = pltpu.get_barrier_semaphore()
    for peer in ctx_peers:
        pl.semaphore_signal(barrier, inc=1, device_id=ctx_peer(peer), device_id_type=MESH)
    for peer in x_peers:
        pl.semaphore_signal(barrier, inc=1, device_id=group_peer(peer), device_id_type=MESH)
    pl.semaphore_wait(barrier, len(ctx_peers) + len(x_peers))

    def remote(chunk, slot, source, target, device):
        copy = pltpu.make_async_remote_copy(
            src_ref=source,
            dst_ref=target,
            send_sem=sends.at[chunk, slot],
            recv_sem=recvs.at[chunk, slot],
            device_id=device,
            device_id_type=MESH,
        )
        copy.start()
        return copy

    def by_rows(rows, step_body):
        block = 32 if rows % 32 == 0 else 16

        def body(index, carry):
            step_body(pl.ds(pl.multiple_of(index * block, block), block))
            return carry

        lax.fori_loop(0, rows // block, body, 0)

    z_slot = depth
    x_slot = z_slot + depth - 1
    zg_slot = x_slot + parts - 1
    yg_slot = zg_slot + depth - 1
    ys, zs, xs, zgs, ygs = ({} for _ in range(5))

    def start_y(c):
        ys[c] = [
            remote(c, z, grads[c].at[2 * z + 1 - side], from_y[c].at[z], ctx_peer(across))
            for z in range(depth)
        ]

    def start_z(c):
        rows = total[c].shape[0]
        for copy in ys[c]:
            copy.wait()

        def add(at):
            for z in range(depth):
                from_y[c][z, at, :] = (
                    grads[c][2 * z + side, at, :].astype(wide) + from_y[c][z, at, :].astype(wide)
                ).astype(low)

        by_rows(rows, add)
        zs[c] = [
            remote(
                c, z_slot + i, from_y[c].at[peer], from_z[c].at[place], ctx_peer(peer * 2 + side)
            )
            for i, peer in enumerate(z_peers)
        ]

    def start_x(c):
        rows = outs[c].shape[1]
        source = grads[c] if ready[c] else total[c]
        for copy in zs.get(c, ()):
            copy.wait()

        def add(at):
            if ready[c]:
                if not turns[c]:
                    outs[c][me, at, :] = grads[c][at, :]
                return
            summed = from_y[c][place, at, :].astype(wide)
            for peer in z_peers:
                summed = summed + from_z[c][peer, at, :].astype(wide)
            if turns[c]:
                total[c][at, :] = summed.astype(low)
            else:
                outs[c][me, at, :] = summed.astype(low)

        if not (ready[c] and turns[c]):
            by_rows(rows, add)
        if turns[c]:
            piece = rows // parts
            xs[c] = [
                remote(
                    c,
                    x_slot + i,
                    source.at[pl.ds(pl.multiple_of(peer * piece, piece), piece)],
                    outs[c].at[me, pl.ds(pl.multiple_of(group_me * piece, piece), piece)],
                    group_peer(peer),
                )
                for i, peer in enumerate(x_peers)
            ]
            mine = pl.ds(pl.multiple_of(group_me * piece, piece), piece)
            outs[c][me, mine, :] = source[mine, :]

    def start_zg(c):
        if turns[c]:
            for copy in xs[c]:
                copy.wait()
        zgs[c] = [
            remote(c, zg_slot + i, outs[c].at[me], outs[c].at[me], ctx_peer(peer * 2 + side))
            for i, peer in enumerate(z_peers)
        ]
        ygs[c] = [remote(c, yg_slot, outs[c].at[me], outs[c].at[me], ctx_peer(across))]

    def start_yg(c):
        for i, (copy, step) in enumerate(zip(zgs[c], range(1, depth))):
            copy.wait()
            came = lax.rem(place + depth - step, depth) * 2 + side
            ygs[c].append(
                remote(c, yg_slot + step, outs[c].at[came], outs[c].at[came], ctx_peer(across))
            )

    gain_copies = []
    for i, peer in enumerate(x_peers):
        gain_copies.append(
            pltpu.make_async_remote_copy(
                src_ref=gains.at[peer],
                dst_ref=gain_in.at[group_me],
                send_sem=gain_sends.at[i],
                recv_sem=gain_recvs.at[i],
                device_id=group_peer(peer),
                device_id_type=MESH,
            )
        )
        gain_copies[-1].start()
    late = [c for c in range(count) if not ready[c]]
    early = [c for c in range(count) if ready[c]]
    for c in late:
        start_y(c)
    for c in early:
        start_x(c)
    start_zg(early[0])
    for copy in gain_copies:
        copy.wait()
    summed = gains[group_me]
    for peer in x_peers:
        summed = summed + gain_in[peer]
    gain_all[me] = summed
    gain_copies = []
    for i, peer in enumerate(ctx_peers):
        gain_copies.append(
            pltpu.make_async_remote_copy(
                src_ref=gain_all.at[me],
                dst_ref=gain_all.at[me],
                send_sem=gain_sends.at[parts - 1 + i],
                recv_sem=gain_recvs.at[parts - 1 + i],
                device_id=ctx_peer(peer),
                device_id_type=MESH,
            )
        )
        gain_copies[-1].start()
    for c in late:
        start_z(c)
    for c in early[1:]:
        start_zg(c)
    for c in late:
        start_x(c)
    start_yg(early[0])
    for c in late:
        start_zg(c)
    for c in early[1:] + late:
        start_yg(c)
    for copy in gain_copies:
        copy.wait()
    summed = gain_all[0]
    for peer in range(1, size):
        summed = summed + gain_all[peer]
    gain_out[...] = summed
    for c in range(count):
        for copy in ygs[c]:
            copy.wait()


def reduce_over_ctx(grads, gains, turns, size, number):
    count = len(grads)
    ready = tuple(g.ndim == 2 for g in grads)
    depth = size // 2
    slots = depth + 2 * (depth - 1) + 3 + depth
    whole = pl.BlockSpec(memory_space=pltpu.VMEM)
    pairs = [
        pltpu.VMEM((1, 16, 128) if g.ndim == 2 else (depth,) + g.shape[1:], g.dtype) for g in grads
    ]
    totals = [pltpu.VMEM((16, 128) if g.ndim == 2 else g.shape[1:], g.dtype) for g in grads]
    return pl.pallas_call(
        functools.partial(reduce_kernel, turns, ready, size, count),
        out_shape=[jax.ShapeDtypeStruct((size,) + g.shape[-2:], g.dtype) for g in grads]
        + [jax.ShapeDtypeStruct(gains.shape[1:], gains.dtype)],
        in_specs=[whole] * (count + 1),
        out_specs=[whole] * (count + 1),
        scratch_shapes=pairs
        + pairs
        + totals
        + [
            pltpu.SemaphoreType.DMA((count, slots)),
            pltpu.SemaphoreType.DMA((count, slots)),
            pltpu.VMEM(gains.shape, gains.dtype),
            pltpu.VMEM((size,) + gains.shape[1:], gains.dtype),
            pltpu.SemaphoreType.DMA((size + 2,)),
            pltpu.SemaphoreType.DMA((size + 2,)),
        ],
        compiler_params=pltpu.CompilerParams(
            collective_id=number, has_side_effects=True, vmem_limit_bytes=48 * 1024 * 1024
        ),
    )(*grads, gains)


def permute_group(chunk_for, parts):
    me = lax.axis_index(GROUP)
    came = [chunk_for(me)]
    for step in range(1, parts):
        pairs = [(i, i ^ step) for i in range(parts)]
        came.append(lax.ppermute(chunk_for(me ^ step), GROUP, pairs))
    return came


def layer_norm_parts(values):
    middle = jnp.mean(values, -1, keepdims=True)
    centred = values - middle
    factor = lax.rsqrt(jnp.mean(centred * centred, -1, keepdims=True) + layer_eps)
    return centred * factor, factor


def norm_back(grad, gain, normed, factor):
    scaled = grad * gain
    return factor * (
        scaled
        - jnp.mean(scaled, -1, keepdims=True)
        - normed * jnp.mean(scaled * normed, -1, keepdims=True)
    )


def dot(equation, left, right):
    return jnp.einsum(equation, left, right, preferred_element_type=jnp.float32)


def parallel(parts, ctx_size, tokens, positions, w_qkv, w_out, w_in, w_down, gain_attn, gain_mlp,
             cotangent):
    low = jnp.bfloat16
    wide = jnp.float32
    row_count = tokens.shape[1]
    length = row_count * ctx_size
    part_heads = HEADS // parts
    part_ff = FF // parts
    part_d = D // parts
    pairs = parts * part_heads // ctx_size
    seq_split = part_heads // pairs
    half = HEAD // 2
    scaling = HEAD ** (-0.5)
    ctx_index = lax.axis_index("ctx")

    gather = square_gather

    def swap_ctx(shard, number):
        return exchange([shard], ctx_size, False, (True,), number)[0]

    inputs = tokens[0].astype(wide)
    cot = cotangent[0]
    small = jnp.concatenate(
        [positions[0].astype(wide), gain_attn.astype(wide), gain_mlp.astype(wide)]
    )
    qkv_split = w_qkv.reshape(part_d, 3, parts, part_d).transpose(2, 0, 1, 3)
    small, all_tokens, qkv_cols = exchange(
        [small.reshape(-1, 128), tokens[0], qkv_split.reshape(parts, part_d, 3 * part_d)],
        parts,
        True,
        (False, False, True),
        1,
    )
    small = small.reshape(parts, -1)
    qkv_cols = qkv_cols.reshape(D, 3 * part_d)
    w_in, cot_sent, small = lax.optimization_barrier((w_in, cot, small))
    gain_one = small[:, row_count : row_count + part_d].reshape(D)
    gain_two = small[:, row_count + part_d :].reshape(D)
    all_positions = (
        exchange([small[:, :row_count].astype(jnp.int32)], ctx_size, False, (False,), 26)[0]
        .transpose(1, 0, 2)
        .reshape(parts, length)
    )
    starts = jnp.arange(length, dtype=jnp.int32)[None, :] - all_positions
    group_positions = lax.dynamic_slice_in_dim(all_positions, ctx_index * row_count, row_count, 1)
    my_seq = ctx_index // seq_split
    seq_positions = lax.dynamic_index_in_dim(all_positions, my_seq, 0, False)
    seq_starts = lax.dynamic_index_in_dim(starts, my_seq, 0, False)

    relative = jnp.arange(parts) ^ lax.axis_index(GROUP)

    def in_chunk(peer):
        return jnp.concatenate(
            [
                lax.dynamic_slice_in_dim(w_in, half_at + peer * part_ff, part_ff, 1)
                for half_at in (0, FF)
            ],
            1,
        )

    in_cols = jnp.concatenate(permute_group(in_chunk, parts))
    all_cot = jnp.stack(permute_group(lambda peer: cot_sent, parts))[relative]
    norm_one, factor_one = layer_norm_parts(inputs)
    normed_attn = (layer_norm_parts(all_tokens.astype(wide))[0] * gain_one).astype(low)
    projected = dot("stc,cf->stf", normed_attn, qkv_cols)
    cosine, sine = rotary_tables(group_positions)
    turned = [
        rotate(
            projected[..., i * part_d : (i + 1) * part_d].reshape(
                parts, row_count, part_heads, HEAD
            ),
            cosine,
            sine,
        )
        for i in range(2)
    ]
    turned.append(projected[..., 2 * part_d :].reshape(parts, row_count, part_heads, HEAD))
    heads_out = jnp.stack([t.astype(low) for t in turned])
    heads_out = (
        heads_out.reshape(3, parts, row_count, seq_split, pairs * HEAD)
        .transpose(1, 3, 2, 0, 4)
        .reshape(ctx_size, row_count, 3 * pairs * HEAD)
    )
    heads_in = swap_ctx(heads_out, 3).reshape(length, 3, pairs, HEAD).transpose(1, 2, 0, 3)
    queries, keys, values = heads_in
    same = (seq_starts[:, None] == seq_starts[None, :])[None]
    scores = jnp.where(same, dot("hqd,hkd->hqk", queries, keys) * scaling, far_below)
    best = jnp.max(scores, -1, keepdims=True)
    raised = jnp.where(same, jnp.exp(scores - best), 0.0)
    totals = jnp.sum(raised, -1, keepdims=True)
    log_total = best + jnp.log(totals)
    attended = dot("hqk,hkd->hqd", raised.astype(low), values) / totals

    def to_tokens(shard, width):
        return (
            shard.transpose(1, 0, 2).reshape(ctx_size, row_count, pairs * width)
        )

    def from_ctx(shard):
        return (
            shard.reshape(parts, seq_split, row_count, -1)
            .transpose(0, 2, 1, 3)
            .reshape(parts, row_count, -1)
        )

    attended_low = from_ctx(swap_ctx(to_tokens(attended.astype(low), HEAD), 4))
    mixed = inputs + square_sum(dot("stc,cf->stf", attended_low, w_out).astype(low), 5)
    norm_two, factor_two = layer_norm_parts(mixed)
    normed_mlp = gather((norm_two * gain_two).astype(low), 6)
    turned_mlp = normed_mlp.reshape(parts, row_count, parts, part_d)[:, :, relative]
    hidden = dot("stc,cf->stf", turned_mlp.reshape(normed_mlp.shape), in_cols)
    inner, gate = hidden[..., :part_ff], hidden[..., part_ff:]
    product, pull = jax.vjp(geglu, inner, gate)
    product = product.astype(low)
    grad_product = dot("stn,fn->stf", all_cot, w_down)
    grad_inner, grad_gate = pull(grad_product)
    grad_hidden = jnp.concatenate([grad_inner, grad_gate], -1).astype(low)
    normed_back = dot("stf,cf->stc", grad_hidden, in_cols).astype(low)
    normed_back = normed_back.reshape(parts, row_count, parts, part_d)[:, :, relative]
    grad_normed_mlp = square_sum(normed_back.reshape(normed_mlp.shape), 9)
    grad_gain_mlp = jnp.sum(grad_normed_mlp * norm_two, 0)
    grad_mixed = cot.astype(wide) + norm_back(grad_normed_mlp, gain_two, norm_two, factor_two)
    grad_branch = gather(grad_mixed.astype(low), 10)
    grad_attended = dot("stf,cf->stc", grad_branch, w_out).astype(low)
    grad_out = (
        grad_attended.reshape(parts, row_count, seq_split, pairs * HEAD)
        .transpose(0, 2, 1, 3)
        .reshape(ctx_size, row_count, pairs * HEAD)
    )
    grad_heads = swap_ctx(grad_out, 11).reshape(length, pairs, HEAD).transpose(1, 0, 2)

    output_parts = dot("stf,fn->stn", product, w_down).astype(low)
    output_parts, grad_branch = lax.optimization_barrier((output_parts, grad_branch))
    output_parts = permute_group(
        lambda peer: lax.dynamic_index_in_dim(output_parts, peer, 0, False), parts
    )
    output = (mixed + sum(part.astype(wide) for part in output_parts)).astype(low)

    def rows_of(grad, width):
        return (
            grad.reshape(parts, ctx_size, part_d // ctx_size, width)
            .transpose(1, 0, 2, 3)
            .reshape(ctx_size, -1, width)
            .astype(low)
        )

    def columns_of(grad):
        rows = grad.shape[0]
        return grad.reshape(rows, ctx_size, D // ctx_size).transpose(1, 0, 2).astype(low)

    def place(grads, pieces):
        specs, shapes = [], []
        for grad, count_of in zip(grads, pieces):
            rows, width = grad.shape[1:]
            if count_of:
                rows, width = part_d // ctx_size, parts * width
                shapes.append((part_d, width))
                specs.append(pl.BlockSpec((rows, width), lambda i: (i, 0)))
            else:
                shapes.append((rows, D))
                specs.append(pl.BlockSpec((rows, width), lambda i: (0, i)))
        return pl.pallas_call(
            functools.partial(place_kernel, parts, pieces),
            grid=(ctx_size,),
            out_shape=[jax.ShapeDtypeStruct(shape, wide) for shape in shapes],
            in_specs=[pl.BlockSpec((1,) + g.shape[1:], lambda i: (i, 0, 0)) for g in grads],
            out_specs=specs,
            compiler_params=pltpu.CompilerParams(vmem_limit_bytes=32 * 1024 * 1024),
        )(*grads)

    depth = ctx_size // 2
    place_z, side = ctx_index // 2, ctx_index % 2

    def sum_sides(grad):
        split = grad.reshape((depth, 2) + grad.shape[1:])
        came = lax.ppermute(
            lax.dynamic_index_in_dim(split, 1 - side, 1, False),
            "ctx",
            [(i, i ^ 1) for i in range(ctx_size)],
        )
        kept = lax.dynamic_index_in_dim(split, side, 1, False)
        return (kept.astype(wide) + came.astype(wide)).astype(low)

    def sum_depth(grad):
        summed = lax.dynamic_index_in_dim(grad, place_z, 0, False).astype(wide)
        for step in range(1, depth):
            summed = summed + lax.ppermute(
                lax.dynamic_index_in_dim(grad, place_z ^ step, 0, False),
                "ctx",
                [(i, i ^ (2 * step)) for i in range(ctx_size)],
            ).astype(wide)
        return summed.astype(low)

    down_grad = sum_sides(columns_of(dot("stf,stn->fn", product, all_cot)))
    in_grad = sum_sides(rows_of(dot("stc,stf->cf", normed_mlp, grad_hidden), 2 * part_ff))
    down_grad = sum_depth(down_grad)
    in_grad = sum_depth(in_grad)

    row_dot = jnp.sum(grad_heads.astype(wide) * attended, -1, keepdims=True)
    weights_f = jnp.where(same, jnp.exp(scores - log_total), 0.0)
    grad_weights = dot("hqd,hkd->hqk", grad_heads, values)
    grad_scores = (weights_f * (grad_weights - row_dot)).astype(low)
    grad_queries = dot("hqk,hkd->hqd", grad_scores, keys) * scaling
    grad_keys = dot("hqk,hqd->hkd", grad_scores, queries) * scaling
    grad_values = dot("hqk,hqd->hkd", weights_f.astype(low), grad_heads)
    seq_cos, seq_sin = rotary_tables(seq_positions)
    seq_cos, seq_sin = seq_cos[:, 0][None], seq_sin[:, 0][None]
    grads = jnp.stack(
        [
            rotate_back(grad_queries, seq_cos, seq_sin),
            rotate_back(grad_keys, seq_cos, seq_sin),
            grad_values,
        ]
    ).astype(low)
    grads = grads.transpose(2, 0, 1, 3).reshape(ctx_size, row_count, 3 * pairs * HEAD)
    down_grad, in_grad, grads = lax.optimization_barrier((down_grad, in_grad, grads))
    grads = swap_ctx(grads, 15)
    grad_projected = (
        grads.reshape(parts, seq_split, row_count, 3, pairs * HEAD)
        .transpose(0, 2, 3, 1, 4)
        .reshape(parts, row_count, 3 * part_d)
    )
    grad_normed_attn = square_sum(dot("stf,cf->stc", grad_projected, qkv_cols).astype(low), 16)
    grad_gain_attn = jnp.sum(grad_normed_attn * norm_one, 0)
    grad_tokens = (
        grad_mixed + norm_back(grad_normed_attn, gain_one, norm_one, factor_one)
    ).astype(low)

    out_grad = columns_of(dot("stc,stf->cf", attended_low, grad_branch))
    qkv_grad = rows_of(dot("stc,stf->cf", normed_attn, grad_projected), 3 * part_d)
    gain_sums = jnp.stack([grad_gain_attn, grad_gain_mlp]).reshape(2, parts, part_d)
    down_grad, in_grad, out_grad, qkv_grad, gain_sums = reduce_over_ctx(
        [down_grad, in_grad, out_grad, qkv_grad],
        gain_sums.transpose(1, 0, 2),
        (False, True, False, True),
        ctx_size,
        13,
    )
    qkv_grad, out_grad, in_grad, down_grad = place(
        [qkv_grad, out_grad, in_grad, down_grad], (3, 0, 2, 0)
    )
    return (
        output[None],
        grad_tokens[None],
        qkv_grad,
        out_grad,
        in_grad,
        down_grad,
        gain_sums[0],
        gain_sums[1],
    )


def solution(mesh):
    placed = (
        P(("seq", "wsh"), "ctx", None),
        P(("seq", "wsh"), "ctx"),
        P(("seq", "wsh"), None),
        P(("seq", "wsh"), None),
        P(("seq", "wsh"), None),
        P(("seq", "wsh"), None),
        P(("seq", "wsh")),
        P(("seq", "wsh")),
        P(("seq", "wsh"), "ctx", None),
    )
    parts = mesh.shape["seq"] * mesh.shape["wsh"]
    ctx_size = mesh.shape["ctx"]
    whole_pairs = HEADS % ctx_size == 0 and ctx_size in (2, 4, 8, 16) and parts == 4
    body = functools.partial(parallel, parts, ctx_size) if whole_pairs else local
    return jax.shard_map(
        body,
        mesh=mesh,
        in_specs=placed,
        out_specs=(
            P(("seq", "wsh"), "ctx", None),
            P(("seq", "wsh"), "ctx", None),
            P(("seq", "wsh"), None),
            P(("seq", "wsh"), None),
            P(("seq", "wsh"), None),
            P(("seq", "wsh"), None),
            P(("seq", "wsh")),
            P(("seq", "wsh")),
        ),
        check_vma=False,
    )
```

```python
import functools
import math

import jax
import jax.numpy as jnp
from jax import lax
from jax.experimental import pallas as pl
from jax.experimental.pallas import tpu as pltpu
from jax.sharding import PartitionSpec as P

D = 1024
HEADS = 16
HEAD = 64
FF = 2624


layer_eps = 1e-05
rope_base = 160000.0
far_below = -1e30


def from_behind(shard, axis, by):
    size = lax.axis_size(axis)
    return lax.ppermute(shard, axis, [(i, (i + by) % size) for i in range(size)])


def normalize(values, gain_vector):
    middle = jnp.mean(values, -1, keepdims=True)
    centred = values - middle
    spread = jnp.mean(centred * centred, -1, keepdims=True)
    return centred * lax.rsqrt(spread + layer_eps) * gain_vector


def rotary_tables(positions):
    half_size = HEAD // 2
    frequency = jnp.exp(
        jnp.arange(half_size, dtype=jnp.float32) * (-2.0 * math.log(rope_base) / HEAD)
    )
    angles = positions.astype(jnp.float32)[..., None] * frequency
    cosine = jnp.cos(angles)
    sine_table = jnp.sin(angles)
    return (
        jnp.concatenate([cosine, cosine], -1)[..., None, :],
        jnp.concatenate([sine_table, sine_table], -1)[..., None, :],
    )


def rotate(values, cosine, sine_table):
    half_size = values.shape[-1] // 2
    turned = jnp.concatenate([-values[..., half_size:], values[..., :half_size]], -1)
    return values * cosine + turned * sine_table


def rotate_back(grads, cosine, sine_table):
    half_size = grads.shape[-1] // 2
    shifted = grads * sine_table
    return grads * cosine + jnp.concatenate(
        [shifted[..., half_size:], -shifted[..., :half_size]], -1
    )


def geglu(inner_part, gate_part):
    return jax.nn.gelu(inner_part, approximate=False) * gate_part


def same_document(query_starts, key_starts):
    return (query_starts[:, :, None] == key_starts[:, None, :])[:, :, None, :]


def fold_keys(queries, query_starts, scaling, running, piece):
    key_piece, value_piece, start_piece = piece
    seq_count = key_piece.shape[0]
    row_total = key_piece.shape[1]
    block_size = math.gcd(row_total, 512)

    def one_block(block_index, carried):
        best_score, totals, weighted = carried
        key_block = lax.dynamic_slice_in_dim(
            key_piece, block_index * block_size, block_size, 1
        ).reshape(seq_count, block_size, HEADS, HEAD)
        value_block = lax.dynamic_slice_in_dim(
            value_piece, block_index * block_size, block_size, 1
        ).reshape(seq_count, block_size, HEADS, HEAD)
        start_block = lax.dynamic_slice_in_dim(start_piece, block_index * block_size, block_size, 1)
        same_doc = same_document(query_starts, start_block)
        scores = (
            jnp.einsum("sqhd,skhd->sqhk", queries, key_block, preferred_element_type=jnp.float32)
            * scaling
        )
        scores = jnp.where(same_doc, scores, far_below)
        new_best = jnp.maximum(best_score, jnp.max(scores, -1))
        fading = jnp.exp(best_score - new_best)
        raised = jnp.where(same_doc, jnp.exp(scores - new_best[..., None]), 0.0)
        totals = totals * fading + jnp.sum(raised, -1)
        weighted = weighted * fading[..., None] + jnp.einsum(
            "sqhk,skhd->sqhd",
            raised.astype(jnp.bfloat16),
            value_block,
            preferred_element_type=jnp.float32,
        )
        return (new_best, totals, weighted)

    return lax.fori_loop(0, row_total // block_size, one_block, running)


def block_grads(
    queries,
    query_starts,
    key_block,
    value_block,
    key_starts,
    grad_split,
    log_total,
    row_dot,
    scaling,
):
    same_doc = same_document(query_starts, key_starts)
    scores = (
        jnp.einsum("sqhd,skhd->sqhk", queries, key_block, preferred_element_type=jnp.float32)
        * scaling
    )
    weights_f = jnp.where(same_doc, jnp.exp(scores - log_total[..., None]), 0.0)
    grad_weights = jnp.einsum(
        "sqhd,skhd->sqhk", grad_split, value_block, preferred_element_type=jnp.float32
    )
    grad_scores = (weights_f * (grad_weights - row_dot[..., None])).astype(jnp.bfloat16)
    grad_query = (
        jnp.einsum("sqhk,skhd->sqhd", grad_scores, key_block, preferred_element_type=jnp.float32)
        * scaling
    )
    grad_key = (
        jnp.einsum("sqhk,sqhd->skhd", grad_scores, queries, preferred_element_type=jnp.float32)
        * scaling
    )
    grad_value = jnp.einsum(
        "sqhk,sqhd->skhd",
        weights_f.astype(jnp.bfloat16),
        grad_split,
        preferred_element_type=jnp.float32,
    )
    return (grad_query, grad_key, grad_value)


def local(tokens, positions, w_qkv, w_out, w_in, w_down, gain_attn, gain_mlp, cotangent):
    seq_count = tokens.shape[0]
    row_count = tokens.shape[1]
    scaling = HEAD ** (-0.5)
    split_shape = (seq_count, row_count, HEADS, HEAD)
    flat_shape = (seq_count, row_count, D)
    (
        forward_query_weight,
        forward_out_weight,
        forward_in_weight,
        forward_down_weight,
        full_ga,
        full_gm,
    ) = (
        lax.all_gather(w_qkv, ("seq", "wsh"), axis=0, tiled=True),
        lax.all_gather(w_out, ("seq", "wsh"), axis=0, tiled=True),
        lax.all_gather(w_in, ("seq", "wsh"), axis=0, tiled=True),
        lax.all_gather(w_down, ("seq", "wsh"), axis=0, tiled=True),
        lax.all_gather(gain_attn, ("seq", "wsh"), axis=0, tiled=True),
        lax.all_gather(gain_mlp, ("seq", "wsh"), axis=0, tiled=True),
    )
    cosine, sine_table = rotary_tables(positions)
    token_index = lax.axis_index("ctx") * row_count + jnp.arange(row_count, dtype=jnp.int32)
    own_starts = token_index[None, :] - positions
    input_widened = tokens.astype(jnp.float32)
    gain_one = full_ga.astype(jnp.float32)
    gain_two = full_gm.astype(jnp.float32)
    attention_normed = normalize(input_widened, gain_one).astype(jnp.bfloat16)
    projected_output = jnp.einsum(
        "kch,hf->kcf", attention_normed, forward_query_weight, preferred_element_type=jnp.float32
    )
    queries = rotate(projected_output[..., :D].reshape(split_shape), cosine, sine_table).astype(
        jnp.bfloat16
    )
    key_rows = (
        rotate(projected_output[..., D : 2 * D].reshape(split_shape), cosine, sine_table)
        .astype(jnp.bfloat16)
        .reshape(flat_shape)
    )
    value_rows = projected_output[..., 2 * D :].astype(jnp.bfloat16)
    start_state = (
        jnp.full((seq_count, row_count, HEADS), far_below, jnp.float32),
        jnp.zeros((seq_count, row_count, HEADS), jnp.float32),
        jnp.zeros(split_shape, jnp.float32),
    )
    best_score, totals, weighted = fold_keys(
        queries,
        own_starts,
        scaling,
        start_state,
        (
            lax.all_gather(key_rows, "ctx", axis=1, tiled=True),
            lax.all_gather(value_rows, "ctx", axis=1, tiled=True),
            lax.all_gather(own_starts, "ctx", axis=1, tiled=True),
        ),
    )
    attended = weighted / totals[..., None]
    log_total = best_score + jnp.log(totals)
    attended_reduced = attended.reshape(flat_shape).astype(jnp.bfloat16)
    mixed_token_rows = input_widened + jnp.einsum(
        "kch,hf->kcf", attended_reduced, forward_out_weight, preferred_element_type=jnp.float32
    )
    feedforward_normed = normalize(mixed_token_rows, gain_two).astype(jnp.bfloat16)
    hidden_state = jnp.einsum(
        "rnk,kx->rnx", feedforward_normed, forward_in_weight, preferred_element_type=jnp.float32
    )
    inner_part = hidden_state[..., :FF]
    gate_part = hidden_state[..., FF:]
    gated_product = geglu(inner_part, gate_part).astype(jnp.bfloat16)
    output = (
        mixed_token_rows
        + jnp.einsum(
            "ogw,wn->ogn", gated_product, forward_down_weight, preferred_element_type=jnp.float32
        )
    ).astype(jnp.bfloat16)
    backward_query_weight, backward_out_weight, backward_in_weight, backward_down_weight = (
        forward_query_weight,
        forward_out_weight,
        forward_in_weight,
        forward_down_weight,
    )
    down_weight_gradient = jnp.einsum(
        "xvt,xvw->tw", gated_product, cotangent, preferred_element_type=jnp.float32
    )
    grad_product = jnp.einsum(
        "xzi,mi->xzm", cotangent, backward_down_weight, preferred_element_type=jnp.float32
    )
    geglu_pull = jax.vjp(geglu, inner_part, gate_part)[1]
    grad_inner, grad_gate = geglu_pull(grad_product)
    hidden_gradient = jnp.concatenate([grad_inner, grad_gate], -1).astype(jnp.bfloat16)
    grad_w_in = jnp.einsum(
        "hrq,hrw->qw", feedforward_normed, hidden_gradient, preferred_element_type=jnp.float32
    )
    grad_normed_mlp = jnp.einsum(
        "xcu,au->xca", hidden_gradient, backward_in_weight, preferred_element_type=jnp.float32
    )
    mlp_pull = jax.vjp(normalize, mixed_token_rows, gain_two)[1]
    grad_mixed_norm, grad_gain_mlp = mlp_pull(grad_normed_mlp)
    grad_mixed = cotangent.astype(jnp.float32) + grad_mixed_norm
    branch_gradient = grad_mixed.astype(jnp.bfloat16)
    grad_w_out = jnp.einsum(
        "pgj,pgv->jv", attended_reduced, branch_gradient, preferred_element_type=jnp.float32
    )
    grad_attended = jnp.einsum(
        "arq,xq->arx", branch_gradient, backward_out_weight, preferred_element_type=jnp.float32
    ).astype(jnp.bfloat16)
    grad_split = grad_attended.reshape(split_shape)
    row_dot = jnp.sum(grad_split.astype(jnp.float32) * attended, -1)
    cycle_turns = lax.axis_size("ctx") - 1
    zeros_flat = jnp.zeros(flat_shape, jnp.float32)

    def key_turn(turn_index, carried):
        moving_keys, moving_values, moving_starts, grad_keys, grad_values, grad_queries = carried
        grad_query, grad_key, grad_value = block_grads(
            queries,
            own_starts,
            moving_keys.reshape(split_shape),
            moving_values.reshape(split_shape),
            moving_starts,
            grad_split,
            log_total,
            row_dot,
            scaling,
        )
        moving_keys, moving_values, moving_starts = from_behind(
            (moving_keys, moving_values, moving_starts), "ctx", 1
        )
        grad_keys, grad_values = (
            from_behind(
                (grad_keys + grad_key.reshape(flat_shape)).astype(jnp.bfloat16), "ctx", 1
            ).astype(jnp.float32),
            from_behind(
                (grad_values + grad_value.reshape(flat_shape)).astype(jnp.bfloat16), "ctx", 1
            ).astype(jnp.float32),
        )
        return (
            moving_keys,
            moving_values,
            moving_starts,
            grad_keys,
            grad_values,
            grad_queries + grad_query,
        )

    moving_keys, moving_values, moving_starts, grad_keys, grad_values, grad_queries = lax.fori_loop(
        0,
        cycle_turns,
        key_turn,
        (
            key_rows,
            value_rows,
            own_starts,
            zeros_flat,
            zeros_flat,
            jnp.zeros(split_shape, jnp.float32),
        ),
    )
    grad_query, grad_key, grad_value = block_grads(
        queries,
        own_starts,
        moving_keys.reshape(split_shape),
        moving_values.reshape(split_shape),
        moving_starts,
        grad_split,
        log_total,
        row_dot,
        scaling,
    )
    grad_queries = grad_queries + grad_query
    grad_keys, grad_values = (
        from_behind(
            (grad_keys + grad_key.reshape(flat_shape)).astype(jnp.bfloat16), "ctx", 1
        ).astype(jnp.float32),
        from_behind(
            (grad_values + grad_value.reshape(flat_shape)).astype(jnp.bfloat16), "ctx", 1
        ).astype(jnp.float32),
    )
    projected_gradient = jnp.concatenate(
        [
            rotate_back(grad_queries, cosine, sine_table).reshape(flat_shape),
            rotate_back(grad_keys.reshape(split_shape), cosine, sine_table).reshape(flat_shape),
            grad_values,
        ],
        -1,
    ).astype(jnp.bfloat16)
    grad_w_qkv = jnp.einsum(
        "pgj,pgv->jv", attention_normed, projected_gradient, preferred_element_type=jnp.float32
    )
    grad_normed_attn = jnp.einsum(
        "arq,xq->arx", projected_gradient, backward_query_weight, preferred_element_type=jnp.float32
    )
    attn_pull = jax.vjp(normalize, input_widened, gain_one)[1]
    grad_inputs_norm, grad_gain_attn = attn_pull(grad_normed_attn)
    grad_tokens = (grad_mixed + grad_inputs_norm).astype(jnp.bfloat16)
    shares = (
        lax.psum_scatter(
            grad_w_qkv.astype(jnp.bfloat16), ("seq", "wsh"), scatter_dimension=0, tiled=True
        ).astype(jnp.float32),
        lax.psum_scatter(
            grad_w_out.astype(jnp.bfloat16), ("seq", "wsh"), scatter_dimension=0, tiled=True
        ).astype(jnp.float32),
        lax.psum_scatter(
            grad_w_in.astype(jnp.bfloat16), ("seq", "wsh"), scatter_dimension=0, tiled=True
        ).astype(jnp.float32),
        lax.psum_scatter(
            down_weight_gradient.astype(jnp.bfloat16),
            ("seq", "wsh"),
            scatter_dimension=0,
            tiled=True,
        ).astype(jnp.float32),
        lax.psum_scatter(
            grad_gain_attn.astype(jnp.bfloat16), ("seq", "wsh"), scatter_dimension=0, tiled=True
        ).astype(jnp.float32),
        lax.psum_scatter(
            grad_gain_mlp.astype(jnp.bfloat16), ("seq", "wsh"), scatter_dimension=0, tiled=True
        ).astype(jnp.float32),
    )
    summed = lax.psum((shares[0], shares[1], shares[2], shares[3], shares[4], shares[5]), "ctx")
    return (output, grad_tokens, summed[0], summed[1], summed[2], summed[3], summed[4], summed[5])


GROUP = ("seq", "wsh")
MESH = pl.DeviceIdType.MESH


def group_peer(index):
    return {"seq": index // 2, "wsh": lax.rem(index, 2)}


def ctx_peer(index):
    return {"ctx": index}


def exchange_kernel(size, group, spreads, *refs):
    count = len(spreads)
    sources, targets = refs[:count], refs[count : 2 * count]
    send_sems, recv_sems, own_sems = refs[2 * count :]
    if group:
        me = lax.axis_index("seq") * 2 + lax.axis_index("wsh")
        peer_of = group_peer
    else:
        me = lax.axis_index("ctx")
        peer_of = ctx_peer
    barrier = pltpu.get_barrier_semaphore()
    for step in range(1, size):
        pl.semaphore_signal(
            barrier, inc=1, device_id=peer_of(lax.rem(me + step, size)), device_id_type=MESH
        )
    pl.semaphore_wait(barrier, size - 1)
    copies = []
    for index, spread in enumerate(spreads):
        src, dst = sources[index], targets[index]
        for step in range(1, size):
            peer = lax.rem(me + step, size)
            copy = pltpu.make_async_remote_copy(
                src_ref=src.at[peer] if spread else src,
                dst_ref=dst.at[me],
                send_sem=send_sems.at[index, step - 1],
                recv_sem=recv_sems.at[index, step - 1],
                device_id=peer_of(peer),
                device_id_type=MESH,
            )
            copy.start()
            copies.append(copy)
        own = pltpu.make_async_copy(src.at[me] if spread else src, dst.at[me], own_sems.at[index])
        own.start()
        copies.append(own)
    for copy in copies:
        copy.wait()


def exchange(shards, size, group, spreads, number):
    count = len(shards)
    return pl.pallas_call(
        functools.partial(exchange_kernel, size, group, spreads),
        out_shape=[
            jax.ShapeDtypeStruct(x.shape if spread else (size,) + x.shape, x.dtype)
            for x, spread in zip(shards, spreads)
        ],
        in_specs=[pl.BlockSpec(memory_space=pl.ANY)] * count,
        out_specs=[pl.BlockSpec(memory_space=pl.ANY)] * count,
        scratch_shapes=[
            pltpu.SemaphoreType.DMA((count, size - 1)),
            pltpu.SemaphoreType.DMA((count, size - 1)),
            pltpu.SemaphoreType.DMA((count,)),
        ],
        compiler_params=pltpu.CompilerParams(collective_id=number, has_side_effects=True),
    )(*shards)


def square_places():
    seq, wsh = lax.axis_index("seq"), lax.axis_index("wsh")
    me = seq * 2 + wsh
    sibling = seq * 2 + 1 - wsh
    across = (1 - seq) * 2 + wsh
    corner = (1 - seq) * 2 + 1 - wsh
    return me, sibling, across, corner


def greet(peers, peer_of):
    barrier = pltpu.get_barrier_semaphore()
    for peer in peers:
        pl.semaphore_signal(barrier, inc=1, device_id=peer_of(peer), device_id_type=MESH)
    pl.semaphore_wait(barrier, len(peers))


def square_copy(source, target, sends, recvs, slot, peer):
    copy = pltpu.make_async_remote_copy(
        src_ref=source,
        dst_ref=target,
        send_sem=sends.at[slot],
        recv_sem=recvs.at[slot],
        device_id=group_peer(peer),
        device_id_type=MESH,
    )
    copy.start()
    return copy


def square_gather_kernel(src, dst, sends, recvs, own_sem):
    me, sibling, across, corner = square_places()
    greet([sibling, across], group_peer)
    far = square_copy(src, dst.at[me], sends, recvs, 0, across)
    near = square_copy(src, dst.at[me], sends, recvs, 1, sibling)
    own = pltpu.make_async_copy(src, dst.at[me], own_sem)
    own.start()
    far.wait()
    onward = square_copy(dst.at[across], dst.at[across], sends, recvs, 2, sibling)
    near.wait()
    own.wait()
    onward.wait()


def square_gather(shard, number):
    whole = pl.BlockSpec(memory_space=pltpu.VMEM)
    return pl.pallas_call(
        square_gather_kernel,
        out_shape=jax.ShapeDtypeStruct((4,) + shard.shape, shard.dtype),
        in_specs=[whole],
        out_specs=whole,
        scratch_shapes=[
            pltpu.SemaphoreType.DMA((3,)),
            pltpu.SemaphoreType.DMA((3,)),
            pltpu.SemaphoreType.DMA,
        ],
        compiler_params=pltpu.CompilerParams(
            collective_id=number, has_side_effects=True, vmem_limit_bytes=32 * 1024 * 1024
        ),
    )(shard)


def square_sum_kernel(src, out, held, sends, recvs):
    wide = jnp.float32
    rows = src.shape[1]
    block = 32 if rows % 32 == 0 else 16
    me, sibling, across, corner = square_places()
    greet([sibling, across], group_peer)
    first = square_copy(src.at[corner], held.at[0], sends, recvs, 0, sibling)
    near = square_copy(src.at[sibling], held.at[1], sends, recvs, 1, sibling)
    first.wait()

    def join(index, carry):
        at = pl.ds(pl.multiple_of(index * block, block), block)
        held[2, at, :] = (src[across, at, :].astype(wide) + held[0, at, :].astype(wide)).astype(
            held.dtype
        )
        return carry

    lax.fori_loop(0, rows // block, join, 0)
    far = square_copy(held.at[2], held.at[3], sends, recvs, 2, across)
    near.wait()
    far.wait()

    def finish(index, carry):
        at = pl.ds(pl.multiple_of(index * block, block), block)
        out[at, :] = (
            src[me, at, :].astype(wide) + held[1, at, :].astype(wide) + held[3, at, :].astype(wide)
        )
        return carry

    lax.fori_loop(0, rows // block, finish, 0)


def square_sum(terms, number):
    whole = pl.BlockSpec(memory_space=pltpu.VMEM)
    return pl.pallas_call(
        square_sum_kernel,
        out_shape=jax.ShapeDtypeStruct(terms.shape[1:], jnp.float32),
        in_specs=[whole],
        out_specs=whole,
        scratch_shapes=[
            pltpu.VMEM(terms.shape, terms.dtype),
            pltpu.SemaphoreType.DMA((3,)),
            pltpu.SemaphoreType.DMA((3,)),
        ],
        compiler_params=pltpu.CompilerParams(
            collective_id=number, has_side_effects=True, vmem_limit_bytes=32 * 1024 * 1024
        ),
    )(terms)


def place_kernel(parts, pieces, *refs):
    count = len(pieces)
    for count_of, grad, out in zip(pieces, refs[:count], refs[count:]):
        if not count_of:
            out[...] = grad[0].astype(out.dtype)
            continue
        rows = out.shape[0]
        width = grad.shape[-1] // count_of
        for piece in range(count_of):
            for part in range(parts):
                start = (piece * parts + part) * width
                out[:, start : start + width] = grad[
                    0, part * rows : (part + 1) * rows, piece * width : (piece + 1) * width
                ].astype(out.dtype)


def reduce_kernel(turns, ready, size, count, *refs):
    low, wide = jnp.bfloat16, jnp.float32
    refs = list(refs)
    gains = refs.pop(count)
    gain_out = refs.pop(2 * count)
    grads, outs = refs[:count], refs[count : 2 * count]
    from_y, from_z, total = (refs[(2 + i) * count : (3 + i) * count] for i in range(3))
    sends, recvs = refs[5 * count : 5 * count + 2]
    gain_in, gain_all, gain_sends, gain_recvs = refs[5 * count + 2 :]
    depth = size // 2
    parts = 4
    me = lax.axis_index("ctx")
    place, side = me // 2, lax.rem(me, 2)
    across = me + 1 - 2 * side
    group_me = lax.axis_index("seq") * 2 + lax.axis_index("wsh")
    z_peers = [lax.rem(place + step, depth) for step in range(1, depth)]
    x_peers = [lax.rem(group_me + step, parts) for step in range(1, parts)]

    ctx_peers = [lax.rem(me + step, size) for step in range(1, size)]
    barrier = pltpu.get_barrier_semaphore()
    for peer in ctx_peers:
        pl.semaphore_signal(barrier, inc=1, device_id=ctx_peer(peer), device_id_type=MESH)
    for peer in x_peers:
        pl.semaphore_signal(barrier, inc=1, device_id=group_peer(peer), device_id_type=MESH)
    pl.semaphore_wait(barrier, len(ctx_peers) + len(x_peers))

    def remote(chunk, slot, source, target, device):
        copy = pltpu.make_async_remote_copy(
            src_ref=source,
            dst_ref=target,
            send_sem=sends.at[chunk, slot],
            recv_sem=recvs.at[chunk, slot],
            device_id=device,
            device_id_type=MESH,
        )
        copy.start()
        return copy

    def by_rows(rows, step_body):
        block = 32 if rows % 32 == 0 else 16

        def body(index, carry):
            step_body(pl.ds(pl.multiple_of(index * block, block), block))
            return carry

        lax.fori_loop(0, rows // block, body, 0)

    z_slot = depth
    x_slot = z_slot + depth - 1
    zg_slot = x_slot + parts - 1
    yg_slot = zg_slot + depth - 1
    ys, zs, xs, zgs, ygs = ({} for _ in range(5))

    def start_y(c):
        ys[c] = [
            remote(c, z, grads[c].at[2 * z + 1 - side], from_y[c].at[z], ctx_peer(across))
            for z in range(depth)
        ]

    def start_z(c):
        rows = total[c].shape[0]
        for copy in ys[c]:
            copy.wait()

        def add(at):
            for z in range(depth):
                from_y[c][z, at, :] = (
                    grads[c][2 * z + side, at, :].astype(wide) + from_y[c][z, at, :].astype(wide)
                ).astype(low)

        by_rows(rows, add)
        zs[c] = [
            remote(
                c, z_slot + i, from_y[c].at[peer], from_z[c].at[place], ctx_peer(peer * 2 + side)
            )
            for i, peer in enumerate(z_peers)
        ]

    def start_x(c):
        rows = outs[c].shape[1]
        source = grads[c] if ready[c] else total[c]
        for copy in zs.get(c, ()):
            copy.wait()

        def add(at):
            if ready[c]:
                if not turns[c]:
                    outs[c][me, at, :] = grads[c][at, :]
                return
            summed = from_y[c][place, at, :].astype(wide)
            for peer in z_peers:
                summed = summed + from_z[c][peer, at, :].astype(wide)
            if turns[c]:
                total[c][at, :] = summed.astype(low)
            else:
                outs[c][me, at, :] = summed.astype(low)

        if not (ready[c] and turns[c]):
            by_rows(rows, add)
        if turns[c]:
            piece = rows // parts
            xs[c] = [
                remote(
                    c,
                    x_slot + i,
                    source.at[pl.ds(pl.multiple_of(peer * piece, piece), piece)],
                    outs[c].at[me, pl.ds(pl.multiple_of(group_me * piece, piece), piece)],
                    group_peer(peer),
                )
                for i, peer in enumerate(x_peers)
            ]
            mine = pl.ds(pl.multiple_of(group_me * piece, piece), piece)
            outs[c][me, mine, :] = source[mine, :]

    def start_zg(c):
        if turns[c]:
            for copy in xs[c]:
                copy.wait()
        zgs[c] = [
            remote(c, zg_slot + i, outs[c].at[me], outs[c].at[me], ctx_peer(peer * 2 + side))
            for i, peer in enumerate(z_peers)
        ]
        ygs[c] = [remote(c, yg_slot, outs[c].at[me], outs[c].at[me], ctx_peer(across))]

    def start_yg(c):
        for i, (copy, step) in enumerate(zip(zgs[c], range(1, depth))):
            copy.wait()
            came = lax.rem(place + depth - step, depth) * 2 + side
            ygs[c].append(
                remote(c, yg_slot + step, outs[c].at[came], outs[c].at[came], ctx_peer(across))
            )

    gain_copies = []
    for i, peer in enumerate(x_peers):
        gain_copies.append(
            pltpu.make_async_remote_copy(
                src_ref=gains.at[peer],
                dst_ref=gain_in.at[group_me],
                send_sem=gain_sends.at[i],
                recv_sem=gain_recvs.at[i],
                device_id=group_peer(peer),
                device_id_type=MESH,
            )
        )
        gain_copies[-1].start()
    late = [c for c in range(count) if not ready[c]]
    early = [c for c in range(count) if ready[c]]
    for c in late:
        start_y(c)
    for c in early:
        start_x(c)
    start_zg(early[0])
    for copy in gain_copies:
        copy.wait()
    summed = gains[group_me]
    for peer in x_peers:
        summed = summed + gain_in[peer]
    gain_all[me] = summed
    gain_copies = []
    for i, peer in enumerate(ctx_peers):
        gain_copies.append(
            pltpu.make_async_remote_copy(
                src_ref=gain_all.at[me],
                dst_ref=gain_all.at[me],
                send_sem=gain_sends.at[parts - 1 + i],
                recv_sem=gain_recvs.at[parts - 1 + i],
                device_id=ctx_peer(peer),
                device_id_type=MESH,
            )
        )
        gain_copies[-1].start()
    for c in late:
        start_z(c)
    for c in early[1:]:
        start_zg(c)
    for c in late:
        start_x(c)
    start_yg(early[0])
    for c in late:
        start_zg(c)
    for c in early[1:] + late:
        start_yg(c)
    for copy in gain_copies:
        copy.wait()
    summed = gain_all[0]
    for peer in range(1, size):
        summed = summed + gain_all[peer]
    gain_out[...] = summed
    for c in range(count):
        for copy in ygs[c]:
            copy.wait()


def reduce_over_ctx(grads, gains, turns, size, number):
    count = len(grads)
    ready = tuple(g.ndim == 2 for g in grads)
    depth = size // 2
    slots = depth + 2 * (depth - 1) + 3 + depth
    whole = pl.BlockSpec(memory_space=pltpu.VMEM)
    pairs = [
        pltpu.VMEM((1, 16, 128) if g.ndim == 2 else (depth,) + g.shape[1:], g.dtype) for g in grads
    ]
    totals = [pltpu.VMEM((16, 128) if g.ndim == 2 else g.shape[1:], g.dtype) for g in grads]
    return pl.pallas_call(
        functools.partial(reduce_kernel, turns, ready, size, count),
        out_shape=[jax.ShapeDtypeStruct((size,) + g.shape[-2:], g.dtype) for g in grads]
        + [jax.ShapeDtypeStruct(gains.shape[1:], gains.dtype)],
        in_specs=[whole] * (count + 1),
        out_specs=[whole] * (count + 1),
        scratch_shapes=pairs
        + pairs
        + totals
        + [
            pltpu.SemaphoreType.DMA((count, slots)),
            pltpu.SemaphoreType.DMA((count, slots)),
            pltpu.VMEM(gains.shape, gains.dtype),
            pltpu.VMEM((size,) + gains.shape[1:], gains.dtype),
            pltpu.SemaphoreType.DMA((size + 2,)),
            pltpu.SemaphoreType.DMA((size + 2,)),
        ],
        compiler_params=pltpu.CompilerParams(
            collective_id=number, has_side_effects=True, vmem_limit_bytes=48 * 1024 * 1024
        ),
    )(*grads, gains)


def permute_group(chunk_for, parts):
    me = lax.axis_index(GROUP)
    came = [chunk_for(me)]
    for step in range(1, parts):
        pairs = [(i, i ^ step) for i in range(parts)]
        came.append(lax.ppermute(chunk_for(me ^ step), GROUP, pairs))
    return came


def layer_norm_parts(values):
    middle = jnp.mean(values, -1, keepdims=True)
    centred = values - middle
    factor = lax.rsqrt(jnp.mean(centred * centred, -1, keepdims=True) + layer_eps)
    return centred * factor, factor


def norm_back(grad, gain, normed, factor):
    scaled = grad * gain
    return factor * (
        scaled
        - jnp.mean(scaled, -1, keepdims=True)
        - normed * jnp.mean(scaled * normed, -1, keepdims=True)
    )


def dot(equation, left, right):
    return jnp.einsum(equation, left, right, preferred_element_type=jnp.float32)


def parallel(parts, ctx_size, tokens, positions, w_qkv, w_out, w_in, w_down, gain_attn, gain_mlp,
             cotangent):
    low = jnp.bfloat16
    wide = jnp.float32
    row_count = tokens.shape[1]
    length = row_count * ctx_size
    part_heads = HEADS // parts
    part_ff = FF // parts
    part_d = D // parts
    pairs = parts * part_heads // ctx_size
    seq_split = part_heads // pairs
    half = HEAD // 2
    scaling = HEAD ** (-0.5)
    ctx_index = lax.axis_index("ctx")

    gather = square_gather

    def swap_ctx(shard, number):
        return exchange([shard], ctx_size, False, (True,), number)[0]

    inputs = tokens[0].astype(wide)
    cot = cotangent[0]
    small = jnp.concatenate(
        [positions[0].astype(wide), gain_attn.astype(wide), gain_mlp.astype(wide)]
    )
    qkv_split = w_qkv.reshape(part_d, 3, parts, part_d).transpose(2, 0, 1, 3)
    small, all_tokens, qkv_cols = exchange(
        [small.reshape(-1, 128), tokens[0], qkv_split.reshape(parts, part_d, 3 * part_d)],
        parts,
        True,
        (False, False, True),
        1,
    )
    small = small.reshape(parts, -1)
    qkv_cols = qkv_cols.reshape(D, 3 * part_d)
    w_in, cot_sent, small = lax.optimization_barrier((w_in, cot, small))
    gain_one = small[:, row_count : row_count + part_d].reshape(D)
    gain_two = small[:, row_count + part_d :].reshape(D)
    all_positions = (
        exchange([small[:, :row_count].astype(jnp.int32)], ctx_size, False, (False,), 26)[0]
        .transpose(1, 0, 2)
        .reshape(parts, length)
    )
    starts = jnp.arange(length, dtype=jnp.int32)[None, :] - all_positions
    group_positions = lax.dynamic_slice_in_dim(all_positions, ctx_index * row_count, row_count, 1)
    my_seq = ctx_index // seq_split
    seq_positions = lax.dynamic_index_in_dim(all_positions, my_seq, 0, False)
    seq_starts = lax.dynamic_index_in_dim(starts, my_seq, 0, False)

    relative = jnp.arange(parts) ^ lax.axis_index(GROUP)

    def in_chunk(peer):
        return jnp.concatenate(
            [
                lax.dynamic_slice_in_dim(w_in, half_at + peer * part_ff, part_ff, 1)
                for half_at in (0, FF)
            ],
            1,
        )

    in_cols = jnp.concatenate(permute_group(in_chunk, parts))
    all_cot = jnp.stack(permute_group(lambda peer: cot_sent, parts))[relative]
    norm_one, factor_one = layer_norm_parts(inputs)
    normed_attn = (layer_norm_parts(all_tokens.astype(wide))[0] * gain_one).astype(low)
    projected = dot("stc,cf->stf", normed_attn, qkv_cols)
    cosine, sine = rotary_tables(group_positions)
    turned = [
        rotate(
            projected[..., i * part_d : (i + 1) * part_d].reshape(
                parts, row_count, part_heads, HEAD
            ),
            cosine,
            sine,
        )
        for i in range(2)
    ]
    turned.append(projected[..., 2 * part_d :].reshape(parts, row_count, part_heads, HEAD))
    heads_out = jnp.stack([t.astype(low) for t in turned])
    heads_out = (
        heads_out.reshape(3, parts, row_count, seq_split, pairs * HEAD)
        .transpose(1, 3, 2, 0, 4)
        .reshape(ctx_size, row_count, 3 * pairs * HEAD)
    )
    heads_in = swap_ctx(heads_out, 3).reshape(length, 3, pairs, HEAD).transpose(1, 2, 0, 3)
    queries, keys, values = heads_in
    same = (seq_starts[:, None] == seq_starts[None, :])[None]
    scores = jnp.where(same, dot("hqd,hkd->hqk", queries, keys) * scaling, far_below)
    best = jnp.max(scores, -1, keepdims=True)
    raised = jnp.where(same, jnp.exp(scores - best), 0.0)
    totals = jnp.sum(raised, -1, keepdims=True)
    log_total = best + jnp.log(totals)
    attended = dot("hqk,hkd->hqd", raised.astype(low), values) / totals

    def to_tokens(shard, width):
        return (
            shard.transpose(1, 0, 2).reshape(ctx_size, row_count, pairs * width)
        )

    def from_ctx(shard):
        return (
            shard.reshape(parts, seq_split, row_count, -1)
            .transpose(0, 2, 1, 3)
            .reshape(parts, row_count, -1)
        )

    attended_low = from_ctx(swap_ctx(to_tokens(attended.astype(low), HEAD), 4))
    mixed = inputs + square_sum(dot("stc,cf->stf", attended_low, w_out).astype(low), 5)
    norm_two, factor_two = layer_norm_parts(mixed)
    normed_mlp = gather((norm_two * gain_two).astype(low), 6)
    turned_mlp = normed_mlp.reshape(parts, row_count, parts, part_d)[:, :, relative]
    hidden = dot("stc,cf->stf", turned_mlp.reshape(normed_mlp.shape), in_cols)
    inner, gate = hidden[..., :part_ff], hidden[..., part_ff:]
    product, pull = jax.vjp(geglu, inner, gate)
    product = product.astype(low)
    grad_product = dot("stn,fn->stf", all_cot, w_down)
    grad_inner, grad_gate = pull(grad_product)
    grad_hidden = jnp.concatenate([grad_inner, grad_gate], -1).astype(low)
    normed_back = dot("stf,cf->stc", grad_hidden, in_cols).astype(low)
    normed_back = normed_back.reshape(parts, row_count, parts, part_d)[:, :, relative]
    def rows_of(grad, width):
        return (
            grad.reshape(parts, ctx_size, part_d // ctx_size, width)
            .transpose(1, 0, 2, 3)
            .reshape(ctx_size, -1, width)
            .astype(low)
        )

    def columns_of(grad):
        rows = grad.shape[0]
        return grad.reshape(rows, ctx_size, D // ctx_size).transpose(1, 0, 2).astype(low)

    depth = ctx_size // 2
    place_z, side = ctx_index // 2, ctx_index % 2

    def by_side(grad):
        split = grad.reshape((depth, 2) + grad.shape[1:])
        return [lax.dynamic_index_in_dim(split, at, 1, False) for at in (side, 1 - side)]

    def sum_sides(kept, sent):
        came = lax.ppermute(sent, "ctx", [(i, i ^ 1) for i in range(ctx_size)])
        return (kept.astype(wide) + came.astype(wide)).astype(low)

    def sum_depth(grad):
        summed = lax.dynamic_index_in_dim(grad, place_z, 0, False).astype(wide)
        for step in range(1, depth):
            summed = summed + lax.ppermute(
                lax.dynamic_index_in_dim(grad, place_z ^ step, 0, False),
                "ctx",
                [(i, i ^ (2 * step)) for i in range(ctx_size)],
            ).astype(wide)
        return summed.astype(low)

    down_kept, down_sent = by_side(columns_of(dot("stf,stn->fn", product, all_cot)))
    in_kept, in_sent = by_side(rows_of(dot("stc,stf->cf", normed_mlp, grad_hidden), 2 * part_ff))
    down_sent, in_sent, normed_back = lax.optimization_barrier((down_sent, in_sent, normed_back))
    down_grad = sum_sides(down_kept, down_sent)
    in_grad = sum_sides(in_kept, in_sent)
    grad_normed_mlp = square_sum(normed_back.reshape(normed_mlp.shape), 9)
    grad_gain_mlp = jnp.sum(grad_normed_mlp * norm_two, 0)
    grad_mixed = cot.astype(wide) + norm_back(grad_normed_mlp, gain_two, norm_two, factor_two)
    down_grad, branch_low = lax.optimization_barrier((down_grad, grad_mixed.astype(low)))
    down_grad = sum_depth(down_grad)
    grad_branch = gather(branch_low, 10)
    grad_attended = dot("stf,cf->stc", grad_branch, w_out).astype(low)
    grad_out = (
        grad_attended.reshape(parts, row_count, seq_split, pairs * HEAD)
        .transpose(0, 2, 1, 3)
        .reshape(ctx_size, row_count, pairs * HEAD)
    )
    grad_heads = swap_ctx(grad_out, 11).reshape(length, pairs, HEAD).transpose(1, 0, 2)

    output_parts = dot("stf,fn->stn", product, w_down).astype(low)
    output_parts, grad_branch = lax.optimization_barrier((output_parts, grad_branch))
    output_parts = permute_group(
        lambda peer: lax.dynamic_index_in_dim(output_parts, peer, 0, False), parts
    )
    output = (mixed + sum(part.astype(wide) for part in output_parts)).astype(low)

    def place(grads, pieces):
        specs, shapes = [], []
        for grad, count_of in zip(grads, pieces):
            rows, width = grad.shape[1:]
            if count_of:
                rows, width = part_d // ctx_size, parts * width
                shapes.append((part_d, width))
                specs.append(pl.BlockSpec((rows, width), lambda i: (i, 0)))
            else:
                shapes.append((rows, D))
                specs.append(pl.BlockSpec((rows, width), lambda i: (0, i)))
        return pl.pallas_call(
            functools.partial(place_kernel, parts, pieces),
            grid=(ctx_size,),
            out_shape=[jax.ShapeDtypeStruct(shape, wide) for shape in shapes],
            in_specs=[pl.BlockSpec((1,) + g.shape[1:], lambda i: (i, 0, 0)) for g in grads],
            out_specs=specs,
            compiler_params=pltpu.CompilerParams(vmem_limit_bytes=32 * 1024 * 1024),
        )(*grads)

    in_grad, down_grad, grad_heads = lax.optimization_barrier((in_grad, down_grad, grad_heads))
    in_grad = sum_depth(in_grad)
    row_dot = jnp.sum(grad_heads.astype(wide) * attended, -1, keepdims=True)
    weights_f = jnp.where(same, jnp.exp(scores - log_total), 0.0)
    grad_weights = dot("hqd,hkd->hqk", grad_heads, values)
    grad_scores = (weights_f * (grad_weights - row_dot)).astype(low)
    grad_queries = dot("hqk,hkd->hqd", grad_scores, keys) * scaling
    grad_keys = dot("hqk,hqd->hkd", grad_scores, queries) * scaling
    grad_values = dot("hqk,hqd->hkd", weights_f.astype(low), grad_heads)
    seq_cos, seq_sin = rotary_tables(seq_positions)
    seq_cos, seq_sin = seq_cos[:, 0][None], seq_sin[:, 0][None]
    grads = jnp.stack(
        [
            rotate_back(grad_queries, seq_cos, seq_sin),
            rotate_back(grad_keys, seq_cos, seq_sin),
            grad_values,
        ]
    ).astype(low)
    grads = grads.transpose(2, 0, 1, 3).reshape(ctx_size, row_count, 3 * pairs * HEAD)
    in_grad, grads = lax.optimization_barrier((in_grad, grads))
    grads = swap_ctx(grads, 15)
    grad_projected = (
        grads.reshape(parts, seq_split, row_count, 3, pairs * HEAD)
        .transpose(0, 2, 3, 1, 4)
        .reshape(parts, row_count, 3 * part_d)
    )
    grad_normed_attn = square_sum(dot("stf,cf->stc", grad_projected, qkv_cols).astype(low), 16)
    grad_gain_attn = jnp.sum(grad_normed_attn * norm_one, 0)
    grad_tokens = (
        grad_mixed + norm_back(grad_normed_attn, gain_one, norm_one, factor_one)
    ).astype(low)

    out_grad = columns_of(dot("stc,stf->cf", attended_low, grad_branch))
    qkv_grad = rows_of(dot("stc,stf->cf", normed_attn, grad_projected), 3 * part_d)
    gain_sums = jnp.stack([grad_gain_attn, grad_gain_mlp]).reshape(2, parts, part_d)
    down_grad, in_grad, out_grad, qkv_grad, gain_sums = reduce_over_ctx(
        [down_grad, in_grad, out_grad, qkv_grad],
        gain_sums.transpose(1, 0, 2),
        (False, True, False, True),
        ctx_size,
        13,
    )
    qkv_grad, out_grad, in_grad, down_grad = place(
        [qkv_grad, out_grad, in_grad, down_grad], (3, 0, 2, 0)
    )
    return (
        output[None],
        grad_tokens[None],
        qkv_grad,
        out_grad,
        in_grad,
        down_grad,
        gain_sums[0],
        gain_sums[1],
    )


def solution(mesh):
    placed = (
        P(("seq", "wsh"), "ctx", None),
        P(("seq", "wsh"), "ctx"),
        P(("seq", "wsh"), None),
        P(("seq", "wsh"), None),
        P(("seq", "wsh"), None),
        P(("seq", "wsh"), None),
        P(("seq", "wsh")),
        P(("seq", "wsh")),
        P(("seq", "wsh"), "ctx", None),
    )
    parts = mesh.shape["seq"] * mesh.shape["wsh"]
    ctx_size = mesh.shape["ctx"]
    whole_pairs = HEADS % ctx_size == 0 and ctx_size in (2, 4, 8, 16) and parts == 4
    body = functools.partial(parallel, parts, ctx_size) if whole_pairs else local
    return jax.shard_map(
        body,
        mesh=mesh,
        in_specs=placed,
        out_specs=(
            P(("seq", "wsh"), "ctx", None),
            P(("seq", "wsh"), "ctx", None),
            P(("seq", "wsh"), None),
            P(("seq", "wsh"), None),
            P(("seq", "wsh"), None),
            P(("seq", "wsh"), None),
            P(("seq", "wsh")),
            P(("seq", "wsh")),
        ),
        check_vma=False,
    )
```
